32 devices in a mesh: tm: 4 (over z), lat: 8 (over y, x, core).
Axes of the slice: x: 2, y: 2, z: 4, core: 2. Of those that a mesh axis runs over, the one named last changes fastest.
Arguments:
- trajectory: float32 [4, 84, 32, 128], P('tm', None, 'lat'), may hold values from -6 to 6
- step_levels: int32 [5], replicated, may hold values from 0 to 63, as said below
- in_weight: bfloat16 [256, 84], replicated, may hold values from -0.625 to 0.625
- in_bias: float32 [256], replicated, may hold values from -4 to 4
- conv_weight: bfloat16 [2, 256, 2304], replicated, may hold values from -0.125 to 0.125
- cond_weight: bfloat16 [256, 1024], replicated, may hold values from -0.375 to 0.375
- out_weight: bfloat16 [84, 256], replicated, may hold values from -0.375 to 0.375
Outputs:
- advanced: float32 [4, 84, 32, 128], P('tm', None, 'lat')
The draws below stay inside these ranges and needn't reach their ends.
Inputs may be any that keep to these rules, and one draw needn't show every extreme that they name: `step_levels`: strictly increasing; the first entry is 0 and the last is 63.
All inputs are finite; a program needn't handle non-finite values.
Results may differ from the reference program's by a relative error of at most 0.0055.
Values may be sent and summed in bfloat16 or wider, within the bound.
A program may use at most 64 MiB of HBM per device.

```python
import jax
import jax.numpy as jnp
from jax import lax

C = 84
HID = 256
EMB = 256
LEVELS = 64
ITERS = 2
W = 128
TIMES = 4
LAT = 32


def draw_step_levels(key, part):
    interior = jax.random.permutation(key, LEVELS - 2)[:TIMES - 1] + 1
    interior = jnp.sort(interior.astype(jnp.int32))
    return jnp.concatenate([jnp.zeros((1,), jnp.int32), interior, jnp.full((1,), LEVELS - 1, jnp.int32)])


def block_levels(own_key, shape, shards, least, largest):
    def one(dim, parts):
        steps = jax.random.uniform(jax.random.fold_in(jax.random.fold_in(own_key, 6), dim), (parts,), jnp.float32, least / len(shards), largest / len(shards))
        return jnp.repeat(jnp.exp(steps), shape[dim] // parts).reshape((-1,) + (1,) * (len(shape) - dim - 1))

    loudness = one(*shards[0])
    for cut in shards[1:]:
        loudness = loudness * one(*cut)
    return loudness


def normal_values(stream_key, dims, scale, most, cuts=(), dtype=jnp.bfloat16):
    array = jax.random.normal(stream_key, dims, jnp.float32) * scale
    if len(cuts) > 0:
        array = block_levels(stream_key, dims, cuts, -0.22, 0.18) * array
    return jnp.clip(array, min=-most, max=most).astype(dtype)


def setup_inputs(seed: int = 0) -> dict:
    key_list = jax.random.split(jax.random.key(seed), 8)
    trajectory = normal_values(key_list[0], (TIMES, C, LAT, W), 1.0, 6.0, ((0, 4), (2, 8)), jnp.float32)
    step_levels = draw_step_levels(jax.random.fold_in(key_list[7], 71), 0)
    in_weight = normal_values(key_list[2], (HID, C), C ** -0.5, 0.625)
    in_bias = normal_values(key_list[3], (HID,), 1.0, 4.0, (), jnp.float32)
    conv_weight = normal_values(key_list[4], (2, HID, 9 * HID), (9 * HID) ** -0.5, 0.125)
    cond_weight = normal_values(key_list[5], (EMB, 4 * HID), EMB ** -0.5, 0.375)
    out_weight = normal_values(key_list[6], (C, HID), HID ** -0.5, 0.375)
    return dict(trajectory=trajectory, step_levels=step_levels, in_weight=in_weight, in_bias=in_bias, conv_weight=conv_weight, cond_weight=cond_weight, out_weight=out_weight)


sigma_top = 1.0
sigma_low = 0.02
rho_power = 7.0

def level_sigma(levels):
    fraction = levels.astype(jnp.float32) / (LEVELS - 1)
    root_value = sigma_top ** (1.0 / rho_power) + fraction * (sigma_low ** (1.0 / rho_power) - sigma_top ** (1.0 / rho_power))
    return root_value ** rho_power

def conditions_of(sigma_now, cond_weight):
    freq_count = EMB // 2
    frequency = 100.0 ** (jnp.arange(freq_count).astype(jnp.float32) / freq_count)
    phases = jnp.log(sigma_now) / 4.0 * frequency
    embedding = jnp.concatenate([jnp.cos(phases), jnp.sin(phases)]).astype(jnp.bfloat16)[None, :]
    conditions = jnp.dot(embedding, cond_weight, preferred_element_type=jnp.float32)[0]
    return jnp.split(conditions, 4)

def convolve(padded, weight):
    row_count = padded.shape[1] - 2
    shifted = []
    for offset_row in range(3):
        for offset_col in (-1, 0, 1):
            shifted.append(jnp.roll(padded[:, offset_row:offset_row + row_count, :], -offset_col, axis=2))
    columns_all = jnp.concatenate(shifted, axis=0)
    channels = columns_all.shape[0]
    flattened = columns_all.reshape(channels, -1)
    response = jnp.dot(weight, flattened, preferred_element_type=jnp.float32)
    return response.reshape(weight.shape[0], row_count, padded.shape[2])

def drift_one(current, sigma_now, sigma_next, in_weight, in_bias, conv_weight, cond_weight, out_weight):
    scale_one, shift_one, scale_two, shift_two = conditions_of(sigma_now, cond_weight)
    variance = sigma_now * sigma_now + 0.25
    scaled = (current / jnp.sqrt(variance)).astype(jnp.bfloat16)
    channels, row_count, columns = current.shape
    hidden_zero = jnp.dot(in_weight, scaled.reshape(channels, -1), preferred_element_type=jnp.float32) + in_bias[:, None]
    hidden_zero = hidden_zero.reshape(-1, row_count, columns).astype(jnp.bfloat16)
    pad_rows = ((0, 0), (1, 1), (0, 0))
    response = convolve(jnp.pad(hidden_zero, pad_rows), conv_weight[0])
    hidden_one = jax.nn.silu(response * (1.0 + scale_one[:, None, None]) + shift_one[:, None, None]).astype(jnp.bfloat16)
    response = convolve(jnp.pad(hidden_one, pad_rows), conv_weight[1])
    hidden_two = hidden_one.astype(jnp.float32) + jax.nn.silu(response * (1.0 + scale_two[:, None, None]) + shift_two[:, None, None])
    hidden_two = hidden_two.astype(jnp.bfloat16)
    network = jnp.dot(out_weight, hidden_two.reshape(hidden_two.shape[0], -1), preferred_element_type=jnp.float32)
    network = network.reshape(channels, row_count, columns)
    denoised = 0.25 / variance * current + 0.5 * sigma_now / jnp.sqrt(variance) * network
    return (current - denoised) * ((sigma_next - sigma_now) / sigma_now)

def reference(trajectory, step_levels, in_weight, in_bias, conv_weight, cond_weight, out_weight):
    sigmas = level_sigma(step_levels)
    sigma_list = sigmas[:-1]
    next_list = sigmas[1:]
    first_state = trajectory[0]

    def all_drifts(states):

        def single(members):
            return drift_one(members[0], members[1], members[2], in_weight, in_bias, conv_weight, cond_weight, out_weight)
        return lax.map(single, (states, sigma_list, next_list))
    states = trajectory
    for sweep in range(ITERS - 1):
        drifts = all_drifts(states)
        summed = first_state[None] + jnp.cumsum(drifts, axis=0)
        states = jnp.concatenate([first_state[None], summed[:-1]], axis=0)
    drifts = all_drifts(states)
    return first_state[None] + jnp.cumsum(drifts, axis=0)
```

```python
import functools

import jax
import jax.numpy as jnp
from jax import lax
from jax.experimental import pallas as pl
from jax.experimental.pallas import tpu as pltpu
from jax.sharding import PartitionSpec as P

LEVELS = 64
MESH = pl.DeviceIdType.MESH

sigma_top = 1.0
sigma_low = 0.02
rho_power = 7.0


def level_sigma(level):
    top, low = sigma_top ** (1.0 / rho_power), sigma_low ** (1.0 / rho_power)
    root = top + level.astype(jnp.float32) / (LEVELS - 1) * (low - top)
    square = root * root
    return square * square * square * root


def kernel(
    sizes,
    levels,
    x_hbm,
    in_hbm,
    bias_hbm,
    conv_hbm,
    cond_hbm,
    out_hbm,
    result,
    xs,
    in_w,
    bias_row,
    conv_w,
    cond_w,
    out_w,
    cond,
    bias,
    g_one,
    g_two,
    drift,
    scaled,
    halo_one,
    recv_one,
    send_one,
    halo_two,
    recv_two,
    send_two,
    load_sem,
    halo_one_s,
    halo_one_r,
    chain_one_s,
    chain_one_r,
    halo_two_s,
    halo_two_r,
    chain_two_s,
    chain_two_r,
):
    times, bands, C, R, W, HID = sizes
    pairs = R // 2
    W2 = 2 * W
    padded = scaled.shape[1]
    slot = lax.axis_index("tm")
    band = lax.axis_index("lat")
    has_low, has_high = band > 0, band < bands - 1
    has_next = slot < times - 1

    loads = [
        pltpu.make_async_copy(source, target, load_sem.at[i])
        for i, (source, target) in enumerate(
            [
                (x_hbm, xs.at[pl.ds(0, C * R)]),
                (in_hbm, in_w),
                (bias_hbm, bias_row),
                (cond_hbm, cond_w),
                (conv_hbm.at[0], conv_w.at[0]),
                (conv_hbm.at[1], conv_w.at[1]),
                (out_hbm, out_w),
            ]
        )
    ]
    for load in loads:
        load.start()

    barrier = pltpu.get_barrier_semaphore()

    def greet(axis, index):
        pl.semaphore_signal(barrier, inc=1, device_id={axis: index}, device_id_type=MESH)

    pl.when(has_low)(lambda: greet("lat", band - 1))
    pl.when(has_high)(lambda: greet("lat", band + 1))
    pl.when(slot > 0)(lambda: greet("tm", slot - 1))

    if padded > C:
        xs[C * R :, :] = jnp.zeros((padded * R - C * R, W), jnp.float32)
    drift[...] = jnp.zeros_like(drift)

    sigma = level_sigma(jnp.full((1, W2), levels[slot], jnp.int32))
    sigma_next = level_sigma(jnp.full((1, W2), levels[slot + 1], jnp.int32))
    variance = sigma * sigma + 0.25
    inverse = 1.0 / jnp.sqrt(variance)
    gain = (sigma_next - sigma) / sigma
    keep = gain * (sigma * sigma / variance)
    push = -0.5 * gain * sigma * inverse

    def own(q):
        return jnp.concatenate(
            [xs[pl.ds(2 * q + i, padded, stride=R), :] for i in range(2)], axis=1
        )

    loads[0].wait()
    for q in range(pairs):
        scaled[q] = (own(q) * inverse).astype(jnp.bfloat16)

    def remote(source, target, send, receive, axis, index):
        return pltpu.make_async_remote_copy(
            src_ref=source,
            dst_ref=target,
            send_sem=send,
            recv_sem=receive,
            device_id={axis: index},
            device_id_type=MESH,
        )

    def down(source, halo, send, receive):
        return remote(source, halo.at[1], send.at[1], receive.at[1], "lat", band - 1)

    def up(source, halo, send, receive):
        return remote(source, halo.at[0], send.at[0], receive.at[0], "lat", band + 1)

    def onward(q, source, target, send, receive):
        return remote(
            source.at[q], target.at[q], send.at[q], receive.at[q], "tm", slot + 1
        )

    first = (halo_one, halo_one_s, halo_one_r)
    second = (halo_two, halo_two_s, halo_two_r)
    chain_one = (send_one, recv_one, chain_one_s, chain_one_r)
    chain_two = (send_two, recv_two, chain_two_s, chain_two_r)

    pl.semaphore_wait(
        barrier,
        has_low.astype(jnp.int32) + has_high.astype(jnp.int32) + has_next.astype(jnp.int32),
    )
    pl.when(has_low)(lambda: down(scaled.at[0], *first).start())
    pl.when(has_high)(lambda: up(scaled.at[pairs - 1], *first).start())

    loads[2].wait()
    for j in range(HID // W):
        rows = pl.ds(j * W, W)
        bias[rows, :] = jnp.broadcast_to(bias_row[:, j * W : (j + 1) * W], (W, W)).T

    half = cond_w.shape[0] // 2
    place = lax.broadcasted_iota(jnp.int32, (1, half), 1).astype(jnp.float32) / half
    frequency = jnp.exp(place * jnp.log(jnp.full((1, half), 100.0, jnp.float32)))
    phases = jnp.log(sigma[:, :1]) / 4.0 * frequency
    embedding = jnp.concatenate([jnp.cos(phases), jnp.sin(phases)], axis=1)
    embedding = jnp.broadcast_to(embedding, (W, 2 * half)).astype(jnp.bfloat16)
    loads[3].wait()
    conditions = jnp.dot(embedding, cond_w[...], preferred_element_type=jnp.float32)
    for j in range(4 * HID // W):
        block = conditions[:, j * W : (j + 1) * W].T
        is_scale = (j * W // HID) % 2 == 0
        cond[pl.ds(j * W, W), :] = block + 1.0 if is_scale else block

    def shifts(target, chunk, halves):
        for i, value in enumerate(halves):
            lanes = pl.ds((2 * chunk + i) * W, W)
            target[pl.ds(0, HID), lanes] = pltpu.roll(value, 1, 1).astype(jnp.bfloat16)
            target[pl.ds(HID, HID), lanes] = value.astype(jnp.bfloat16)
            target[pl.ds(2 * HID, HID), lanes] = pltpu.roll(value, W - 1, 1).astype(jnp.bfloat16)

    def project(chunk, value, inside=None):
        hidden = jnp.dot(in_w[...], value, preferred_element_type=jnp.float32)
        halves = []
        for i in range(2):
            part = hidden[:, i * W : (i + 1) * W] + bias[...]
            halves.append(part if inside is None else jnp.where(inside, part, 0.0))
        shifts(g_one, chunk, halves)

    def convolve(source, layer, pair):
        total = None
        for a in range(3):
            term = jnp.dot(
                conv_w[layer, :, a * 3 * HID : (a + 1) * 3 * HID],
                source[:, (2 * pair + a) * W : (2 * pair + a + 2) * W],
                preferred_element_type=jnp.float32,
            )
            total = term if total is None else total + term
        return total

    def activated(response, layer, i):
        scale = cond[pl.ds(2 * layer * HID, HID), :]
        shift = cond[pl.ds((2 * layer + 1) * HID, HID), :]
        value = response[:, i * W : (i + 1) * W] * scale + shift
        part = 0.5 * value
        return part + part * jnp.tanh(part)

    def layer_one(pair):
        response = convolve(g_one, 0, pair)
        halves = [activated(response, 0, i) for i in range(2)]
        if pair == 0:
            halves[0] = jnp.where(has_low, halves[0], 0.0)
        if pair == pairs:
            halves[1] = jnp.where(has_high, halves[1], 0.0)
        shifts(g_two, pair, halves)

    def layer_two(pair, current):
        response = convolve(g_two, 1, pair)
        halves = []
        for i in range(2):
            lanes = pl.ds((2 * pair + 1 + i) * W, W)
            carried = g_two[pl.ds(HID, HID), lanes].astype(jnp.float32)
            halves.append((carried + activated(response, 1, i)).astype(jnp.bfloat16))
        network = jnp.dot(
            out_w[...], jnp.concatenate(halves, axis=1), preferred_element_type=jnp.float32
        )
        drift[pair, 0:C, :] = push * network
        return keep * current + drift[pair]

    def write(pair, value):
        for i in range(2):
            result[pl.ds(2 * pair + i, C, stride=R), :] = value[0:C, i * W : (i + 1) * W]

    loads[1].wait()
    for q in range(pairs):
        project(q + 1, scaled[q, 0:C, :])
    loads[4].wait()
    for pair in range(1, pairs):
        layer_one(pair)
    pl.when(has_low)(lambda: up(scaled.at[pairs - 1], *first).wait_recv())
    project(0, halo_one[0, 0:C, :], has_low)
    layer_one(0)
    loads[5].wait()
    loads[6].wait()
    for q in range(pairs):
        if q == pairs - 1:
            pl.when(has_high)(lambda: down(scaled.at[0], *first).wait_recv())
            project(pairs + 1, halo_one[1, 0:C, :], has_high)
            layer_one(pairs)
        current = own(q)
        change = layer_two(q, current)

        @pl.when(slot == 0)
        def _():
            total = current + change
            write(q, total)
            send_one[q] = total.astype(jnp.bfloat16)

        @pl.when(slot > 0)
        def _():
            onward(q, *chain_one).wait_recv()
            if q == 0:
                pl.when(has_low)(lambda: down(recv_one.at[0], *second).start())
            if q == pairs - 1:
                pl.when(has_high)(lambda: up(recv_one.at[pairs - 1], *second).start())
            send_one[q] = (recv_one[q].astype(jnp.float32) + change).astype(jnp.bfloat16)

        pl.when(has_next)(lambda: onward(q, *chain_one).start())

    @pl.when(slot > 0)
    def _():
        def state(q):
            return recv_one[q].astype(jnp.float32)

        def rescaled(value):
            return (value[0:C].astype(jnp.float32) * inverse).astype(jnp.bfloat16)

        for q in range(pairs):
            project(q + 1, rescaled(recv_one[q]))
        for pair in range(1, pairs):
            layer_one(pair)
        pl.when(has_high)(lambda: down(recv_one.at[0], *second).wait_recv())
        project(pairs + 1, rescaled(halo_two[1]), has_high)
        layer_one(pairs)
        for q in reversed(range(pairs)):
            if q == 0:
                pl.when(has_low)(lambda: up(recv_one.at[pairs - 1], *second).wait_recv())
                project(0, rescaled(halo_two[0]), has_low)
                layer_one(0)
            current = state(q)
            change = layer_two(q, current)

            @pl.when(slot == 1)
            def _():
                total = current + change
                write(q, total)
                send_two[q] = total.astype(jnp.bfloat16)

            @pl.when(slot > 1)
            def _():
                onward(q, *chain_two).wait_recv()
                total = recv_two[q].astype(jnp.float32) + change
                write(q, total)
                send_two[q] = total.astype(jnp.bfloat16)

            pl.when(has_next)(lambda: onward(q, *chain_two).start())

    pl.when(has_low)(lambda: down(scaled.at[0], *first).wait_send())
    pl.when(has_high)(lambda: up(scaled.at[pairs - 1], *first).wait_send())

    @pl.when(has_next)
    def _():
        for q in range(pairs):
            onward(q, *chain_one).wait_send()

    @pl.when(slot > 0)
    def _():
        pl.when(has_low)(lambda: down(recv_one.at[0], *second).wait_send())
        pl.when(has_high)(lambda: up(recv_one.at[pairs - 1], *second).wait_send())

        @pl.when(has_next)
        def _():
            for q in range(pairs):
                onward(q, *chain_two).wait_send()


def on_device(times, bands, trajectory, step_levels, in_weight, in_bias, conv_weight, cond_weight, out_weight):
    _, C, R, W = trajectory.shape
    HID = in_weight.shape[0]
    pairs = R // 2
    padded = -(-C // 16) * 16
    bf16, f32 = jnp.bfloat16, jnp.float32
    block = (pairs, padded, 2 * W)
    halo = (2, padded, 2 * W)
    anywhere = pl.BlockSpec(memory_space=pl.ANY)
    dma = pltpu.SemaphoreType.DMA
    result = pl.pallas_call(
        functools.partial(kernel, (times, bands, C, R, W, HID)),
        out_shape=jax.ShapeDtypeStruct((C * R, W), f32),
        in_specs=[pl.BlockSpec(memory_space=pltpu.SMEM)] + [anywhere] * 6,
        out_specs=pl.BlockSpec(memory_space=pltpu.VMEM),
        scratch_shapes=[
            pltpu.VMEM((padded * R, W), f32),
            pltpu.VMEM(in_weight.shape, bf16),
            pltpu.VMEM((1, HID), f32),
            pltpu.VMEM(conv_weight.shape, bf16),
            pltpu.VMEM(cond_weight.shape, bf16),
            pltpu.VMEM(out_weight.shape, bf16),
            pltpu.VMEM((4 * HID, W), f32),
            pltpu.VMEM((HID, W), f32),
            pltpu.VMEM((3 * HID, (R + 4) * W), bf16),
            pltpu.VMEM((3 * HID, (R + 2) * W), bf16),
            pltpu.VMEM(block, f32),
            pltpu.VMEM(block, bf16),
            pltpu.VMEM(halo, bf16),
            pltpu.VMEM(block, bf16),
            pltpu.VMEM(block, bf16),
            pltpu.VMEM(halo, bf16),
            pltpu.VMEM(block, bf16),
            pltpu.VMEM(block, bf16),
            dma((7,)),
            dma((2,)),
            dma((2,)),
            dma((pairs,)),
            dma((pairs,)),
            dma((2,)),
            dma((2,)),
            dma((pairs,)),
            dma((pairs,)),
        ],
        compiler_params=pltpu.CompilerParams(
            collective_id=0, has_side_effects=True, vmem_limit_bytes=32 * 1024 * 1024
        ),
    )(
        step_levels,
        trajectory.reshape(C * R, W),
        in_weight,
        in_bias.reshape(1, HID),
        conv_weight,
        cond_weight,
        out_weight,
    )
    return result.reshape(1, C, R, W)


def solution(mesh):
    in_specs = (P("tm", None, "lat", None), P(), P(), P(), P(), P(), P())
    out_specs = P("tm", None, "lat", None)
    return jax.shard_map(
        functools.partial(on_device, mesh.shape["tm"], mesh.shape["lat"]),
        mesh=mesh,
        in_specs=in_specs,
        out_specs=out_specs,
        check_vma=False,
    )
```

```python
import functools

import jax
import jax.numpy as jnp
from jax import lax
from jax.experimental import pallas as pl
from jax.experimental.pallas import tpu as pltpu
from jax.sharding import PartitionSpec as P

LEVELS = 64
MESH = pl.DeviceIdType.MESH

sigma_top = 1.0
sigma_low = 0.02
rho_power = 7.0


def level_sigma(level):
    top, low = sigma_top ** (1.0 / rho_power), sigma_low ** (1.0 / rho_power)
    root = top + level.astype(jnp.float32) / (LEVELS - 1) * (low - top)
    square = root * root
    return square * square * square * root


def kernel(
    sizes,
    levels,
    x_hbm,
    in_hbm,
    bias_hbm,
    conv_hbm,
    cond_hbm,
    out_hbm,
    result,
    xs,
    in_t,
    in_pad,
    in_w,
    bias_row,
    conv_w,
    cond_w,
    out_w,
    cond,
    bias,
    g_one,
    g_two,
    drift,
    scaled,
    halo_one,
    recv_one,
    send_one,
    halo_two,
    recv_two,
    send_two,
    load_sem,
    halo_one_s,
    halo_one_r,
    chain_one_s,
    chain_one_r,
    halo_two_s,
    halo_two_r,
    chain_two_s,
    chain_two_r,
):
    times, bands, C, R, W, HID = sizes
    pairs = R // 2
    W2 = 2 * W
    padded = scaled.shape[1]
    slot = lax.axis_index("tm")
    band = lax.axis_index("lat")
    has_low, has_high = band > 0, band < bands - 1
    has_next = slot < times - 1

    loads = [
        pltpu.make_async_copy(source, target, load_sem.at[i])
        for i, (source, target) in enumerate(
            [
                (x_hbm, xs.at[pl.ds(0, C * R)]),
                (in_hbm, in_t),
                (bias_hbm, bias_row),
                (cond_hbm, cond_w),
                (conv_hbm.at[0], conv_w.at[0]),
                (conv_hbm.at[1], conv_w.at[1]),
                (out_hbm, out_w),
            ]
        )
    ]
    for load in loads:
        load.start()

    barrier = pltpu.get_barrier_semaphore()

    def greet(axis, index):
        pl.semaphore_signal(barrier, inc=1, device_id={axis: index}, device_id_type=MESH)

    pl.when(has_low)(lambda: greet("lat", band - 1))
    pl.when(has_high)(lambda: greet("lat", band + 1))
    pl.when(slot > 0)(lambda: greet("tm", slot - 1))

    if padded > C:
        xs[C * R :, :] = jnp.zeros((padded * R - C * R, W), jnp.float32)
    drift[...] = jnp.zeros_like(drift)

    sigma = level_sigma(jnp.full((1, W2), levels[slot], jnp.int32))
    sigma_next = level_sigma(jnp.full((1, W2), levels[slot + 1], jnp.int32))
    variance = sigma * sigma + 0.25
    inverse = 1.0 / jnp.sqrt(variance)
    gain = (sigma_next - sigma) / sigma
    keep = gain * (sigma * sigma / variance)
    push = -0.5 * gain * sigma * inverse

    def own(q):
        return jnp.concatenate(
            [xs[pl.ds(2 * q + i, padded, stride=R), :] for i in range(2)], axis=1
        )

    loads[0].wait()
    for q in range(pairs):
        scaled[q] = (own(q) * inverse).astype(jnp.bfloat16)

    def remote(source, target, send, receive, axis, index):
        return pltpu.make_async_remote_copy(
            src_ref=source,
            dst_ref=target,
            send_sem=send,
            recv_sem=receive,
            device_id={axis: index},
            device_id_type=MESH,
        )

    def down(source, halo, send, receive):
        return remote(source, halo.at[1], send.at[1], receive.at[1], "lat", band - 1)

    def up(source, halo, send, receive):
        return remote(source, halo.at[0], send.at[0], receive.at[0], "lat", band + 1)

    def onward(q, source, target, send, receive):
        return remote(
            source.at[q], target.at[q], send.at[q], receive.at[q], "tm", slot + 1
        )

    first = (halo_one, halo_one_s, halo_one_r)
    second = (halo_two, halo_two_s, halo_two_r)
    chain_one = (send_one, recv_one, chain_one_s, chain_one_r)
    chain_two = (send_two, recv_two, chain_two_s, chain_two_r)

    pl.semaphore_wait(
        barrier,
        has_low.astype(jnp.int32) + has_high.astype(jnp.int32) + has_next.astype(jnp.int32),
    )
    pl.when(has_low)(lambda: down(scaled.at[0], *first).start())
    pl.when(has_high)(lambda: up(scaled.at[pairs - 1], *first).start())

    in_pad[...] = jnp.zeros_like(in_pad)
    loads[1].wait()
    loads[2].wait()
    in_pad[0:C, :] = in_t[...].astype(jnp.float32)
    for j in range(HID // W):
        rows = pl.ds(j * W, W)
        in_w[rows, :] = in_pad[:, j * W : (j + 1) * W].T.astype(jnp.bfloat16)
        bias[rows, :] = jnp.broadcast_to(bias_row[:, j * W : (j + 1) * W], (W, W)).T

    half = cond_w.shape[0] // 2
    place = lax.broadcasted_iota(jnp.int32, (1, half), 1).astype(jnp.float32) / half
    frequency = jnp.exp(place * jnp.log(jnp.full((1, half), 100.0, jnp.float32)))
    phases = jnp.log(sigma[:, :1]) / 4.0 * frequency
    embedding = jnp.concatenate([jnp.cos(phases), jnp.sin(phases)], axis=1)
    embedding = jnp.broadcast_to(embedding, (W, 2 * half)).astype(jnp.bfloat16)
    loads[3].wait()
    conditions = jnp.dot(embedding, cond_w[...], preferred_element_type=jnp.float32)
    for j in range(4 * HID // W):
        block = conditions[:, j * W : (j + 1) * W].T
        is_scale = (j * W // HID) % 2 == 0
        cond[pl.ds(j * W, W), :] = block + 1.0 if is_scale else block

    def shifts(target, chunk, halves):
        for i, value in enumerate(halves):
            lanes = pl.ds((2 * chunk + i) * W, W)
            target[pl.ds(0, HID), lanes] = pltpu.roll(value, 1, 1).astype(jnp.bfloat16)
            target[pl.ds(HID, HID), lanes] = value.astype(jnp.bfloat16)
            target[pl.ds(2 * HID, HID), lanes] = pltpu.roll(value, W - 1, 1).astype(jnp.bfloat16)

    def project(chunk, value, inside=None):
        hidden = jnp.dot(in_w[:, :padded], value, preferred_element_type=jnp.float32)
        halves = []
        for i in range(2):
            part = hidden[:, i * W : (i + 1) * W] + bias[...]
            halves.append(part if inside is None else jnp.where(inside, part, 0.0))
        shifts(g_one, chunk, halves)

    def convolve(source, layer, pair):
        total = None
        for a in range(3):
            term = jnp.dot(
                conv_w[layer, :, a * 3 * HID : (a + 1) * 3 * HID],
                source[:, (2 * pair + a) * W : (2 * pair + a + 2) * W],
                preferred_element_type=jnp.float32,
            )
            total = term if total is None else total + term
        return total

    def activated(response, layer, i):
        scale = cond[pl.ds(2 * layer * HID, HID), :]
        shift = cond[pl.ds((2 * layer + 1) * HID, HID), :]
        value = response[:, i * W : (i + 1) * W] * scale + shift
        part = 0.5 * value
        return part + part * jnp.tanh(part)

    def layer_one(pair):
        response = convolve(g_one, 0, pair)
        halves = [activated(response, 0, i) for i in range(2)]
        if pair == 0:
            halves[0] = jnp.where(has_low, halves[0], 0.0)
        if pair == pairs:
            halves[1] = jnp.where(has_high, halves[1], 0.0)
        shifts(g_two, pair, halves)

    def layer_two(pair, current):
        response = convolve(g_two, 1, pair)
        halves = []
        for i in range(2):
            lanes = pl.ds((2 * pair + 1 + i) * W, W)
            carried = g_two[pl.ds(HID, HID), lanes].astype(jnp.float32)
            halves.append((carried + activated(response, 1, i)).astype(jnp.bfloat16))
        network = jnp.dot(
            out_w[...], jnp.concatenate(halves, axis=1), preferred_element_type=jnp.float32
        )
        drift[pair, 0:C, :] = push * network
        return keep * current + drift[pair]

    def write(pair, value):
        for i in range(2):
            result[pl.ds(2 * pair + i, C, stride=R), :] = value[0:C, i * W : (i + 1) * W]

    for q in range(pairs):
        project(q + 1, scaled[q])
    loads[4].wait()
    for pair in range(1, pairs):
        layer_one(pair)
    pl.when(has_low)(lambda: up(scaled.at[pairs - 1], *first).wait_recv())
    project(0, halo_one[0], has_low)
    layer_one(0)
    loads[5].wait()
    loads[6].wait()
    for q in range(pairs):
        if q == pairs - 1:
            pl.when(has_high)(lambda: down(scaled.at[0], *first).wait_recv())
            project(pairs + 1, halo_one[1], has_high)
            layer_one(pairs)
        current = own(q)
        change = layer_two(q, current)

        @pl.when(slot == 0)
        def _():
            total = current + change
            write(q, total)
            send_one[q] = total.astype(jnp.bfloat16)

        @pl.when(slot > 0)
        def _():
            onward(q, *chain_one).wait_recv()
            if q == 0:
                pl.when(has_low)(lambda: down(recv_one.at[0], *second).start())
            if q == pairs - 1:
                pl.when(has_high)(lambda: up(recv_one.at[pairs - 1], *second).start())
            send_one[q] = (recv_one[q].astype(jnp.float32) + change).astype(jnp.bfloat16)

        pl.when(has_next)(lambda: onward(q, *chain_one).start())

    @pl.when(slot > 0)
    def _():
        def state(q):
            return recv_one[q].astype(jnp.float32)

        def rescaled(value):
            return (value.astype(jnp.float32) * inverse).astype(jnp.bfloat16)

        for q in range(pairs):
            project(q + 1, rescaled(recv_one[q]))
        for pair in range(1, pairs):
            layer_one(pair)
        pl.when(has_high)(lambda: down(recv_one.at[0], *second).wait_recv())
        project(pairs + 1, rescaled(halo_two[1]), has_high)
        layer_one(pairs)
        for q in reversed(range(pairs)):
            if q == 0:
                pl.when(has_low)(lambda: up(recv_one.at[pairs - 1], *second).wait_recv())
                project(0, rescaled(halo_two[0]), has_low)
                layer_one(0)
            current = state(q)
            change = layer_two(q, current)

            @pl.when(slot == 1)
            def _():
                total = current + change
                write(q, total)
                send_two[q] = total.astype(jnp.bfloat16)

            @pl.when(slot > 1)
            def _():
                onward(q, *chain_two).wait_recv()
                total = recv_two[q].astype(jnp.float32) + change
                write(q, total)
                send_two[q] = total.astype(jnp.bfloat16)

            pl.when(has_next)(lambda: onward(q, *chain_two).start())

    pl.when(has_low)(lambda: down(scaled.at[0], *first).wait_send())
    pl.when(has_high)(lambda: up(scaled.at[pairs - 1], *first).wait_send())

    @pl.when(has_next)
    def _():
        for q in range(pairs):
            onward(q, *chain_one).wait_send()

    @pl.when(slot > 0)
    def _():
        pl.when(has_low)(lambda: down(recv_one.at[0], *second).wait_send())
        pl.when(has_high)(lambda: up(recv_one.at[pairs - 1], *second).wait_send())

        @pl.when(has_next)
        def _():
            for q in range(pairs):
                onward(q, *chain_two).wait_send()


def on_device(times, bands, trajectory, step_levels, in_weight, in_bias, conv_weight, cond_weight, out_weight):
    _, C, R, W = trajectory.shape
    HID = in_weight.shape[0]
    pairs = R // 2
    padded = -(-C // 16) * 16
    wide = -(-C // 128) * 128
    bf16, f32 = jnp.bfloat16, jnp.float32
    block = (pairs, padded, 2 * W)
    halo = (2, padded, 2 * W)
    anywhere = pl.BlockSpec(memory_space=pltpu.HBM)
    dma = pltpu.SemaphoreType.DMA
    result = pl.pallas_call(
        functools.partial(kernel, (times, bands, C, R, W, HID)),
        out_shape=jax.ShapeDtypeStruct((C * R, W), f32),
        in_specs=[pl.BlockSpec(memory_space=pltpu.SMEM)] + [anywhere] * 6,
        out_specs=pl.BlockSpec(memory_space=pltpu.VMEM),
        scratch_shapes=[
            pltpu.VMEM((padded * R, W), f32),
            pltpu.VMEM((C, HID), bf16),
            pltpu.VMEM((wide, HID), f32),
            pltpu.VMEM((HID, wide), bf16),
            pltpu.VMEM((1, HID), f32),
            pltpu.VMEM(conv_weight.shape, bf16),
            pltpu.VMEM(cond_weight.shape, bf16),
            pltpu.VMEM(out_weight.shape, bf16),
            pltpu.VMEM((4 * HID, W), f32),
            pltpu.VMEM((HID, W), f32),
            pltpu.VMEM((3 * HID, (R + 4) * W), bf16),
            pltpu.VMEM((3 * HID, (R + 2) * W), bf16),
            pltpu.VMEM(block, f32),
            pltpu.VMEM(block, bf16),
            pltpu.VMEM(halo, bf16),
            pltpu.VMEM(block, bf16),
            pltpu.VMEM(block, bf16),
            pltpu.VMEM(halo, bf16),
            pltpu.VMEM(block, bf16),
            pltpu.VMEM(block, bf16),
            dma((7,)),
            dma((2,)),
            dma((2,)),
            dma((pairs,)),
            dma((pairs,)),
            dma((2,)),
            dma((2,)),
            dma((pairs,)),
            dma((pairs,)),
        ],
        compiler_params=pltpu.CompilerParams(
            collective_id=0, has_side_effects=True, vmem_limit_bytes=60 * 1024 * 1024
        ),
    )(
        step_levels,
        trajectory.reshape(C * R, W),
        in_weight.T,
        in_bias.reshape(1, HID),
        conv_weight,
        cond_weight,
        out_weight,
    )
    return result.reshape(1, C, R, W)


def solution(mesh):
    in_specs = (P("tm", None, "lat", None), P(), P(), P(), P(), P(), P())
    out_specs = P("tm", None, "lat", None)
    return jax.shard_map(
        functools.partial(on_device, mesh.shape["tm"], mesh.shape["lat"]),
        mesh=mesh,
        in_specs=in_specs,
        out_specs=out_specs,
        check_vma=False,
    )
```

```python
import functools

import jax
import jax.numpy as jnp
from jax import lax
from jax.experimental import pallas as pl
from jax.experimental.pallas import tpu as pltpu
from jax.sharding import PartitionSpec as P

LEVELS = 64
MESH = pl.DeviceIdType.MESH

sigma_top = 1.0
sigma_low = 0.02
rho_power = 7.0


def level_sigma(level):
    top, low = sigma_top ** (1.0 / rho_power), sigma_low ** (1.0 / rho_power)
    root = top + level.astype(jnp.float32) / (LEVELS - 1) * (low - top)
    square = root * root
    return square * square * square * root


def kernel(
    sizes,
    levels_hbm,
    x_hbm,
    in_hbm,
    bias_hbm,
    conv_hbm,
    cond_hbm,
    out_hbm,
    result,
    levels,
    xs,
    in_t,
    in_pad,
    in_w,
    bias_row,
    conv_w,
    cond_w,
    out_w,
    cond,
    bias,
    g_one,
    g_two,
    drift,
    scaled,
    halo_one,
    recv_one,
    send_one,
    halo_two,
    recv_two,
    send_two,
    load_sem,
    halo_one_s,
    halo_one_r,
    chain_one_s,
    chain_one_r,
    halo_two_s,
    halo_two_r,
    chain_two_s,
    chain_two_r,
):
    times, bands, C, R, W, HID = sizes
    pairs = R // 2
    W2 = 2 * W
    padded = scaled.shape[1]
    slot = lax.axis_index("tm")
    band = lax.axis_index("lat")
    has_low, has_high = band > 0, band < bands - 1
    has_next = slot < times - 1

    loads = [
        pltpu.make_async_copy(source, target, load_sem.at[i])
        for i, (source, target) in enumerate(
            [
                (x_hbm, xs.at[pl.ds(0, C * R)]),
                (in_hbm, in_t),
                (bias_hbm, bias_row),
                (cond_hbm, cond_w),
                (conv_hbm.at[0], conv_w.at[0]),
                (conv_hbm.at[1], conv_w.at[1]),
                (out_hbm, out_w),
                (levels_hbm, levels),
            ]
        )
    ]
    for load in loads[-1:] + loads[:-1]:
        load.start()

    barrier = pltpu.get_barrier_semaphore()

    def greet(axis, index):
        pl.semaphore_signal(barrier, inc=1, device_id={axis: index}, device_id_type=MESH)

    pl.when(has_low)(lambda: greet("lat", band - 1))
    pl.when(has_high)(lambda: greet("lat", band + 1))
    pl.when(slot > 0)(lambda: greet("tm", slot - 1))

    if padded > C:
        xs[C * R :, :] = jnp.zeros((padded * R - C * R, W), jnp.float32)
    drift[...] = jnp.zeros_like(drift)

    loads[7].wait()
    sigma = level_sigma(jnp.full((1, W2), levels[slot], jnp.int32))
    sigma_next = level_sigma(jnp.full((1, W2), levels[slot + 1], jnp.int32))
    variance = sigma * sigma + 0.25
    inverse = 1.0 / jnp.sqrt(variance)
    gain = (sigma_next - sigma) / sigma
    keep = gain * (sigma * sigma / variance)
    push = -0.5 * gain * sigma * inverse

    def own(q):
        return jnp.concatenate(
            [xs[pl.ds(2 * q + i, padded, stride=R), :] for i in range(2)], axis=1
        )

    loads[0].wait()
    for q in range(pairs):
        scaled[q] = (own(q) * inverse).astype(jnp.bfloat16)

    def remote(source, target, send, receive, axis, index):
        return pltpu.make_async_remote_copy(
            src_ref=source,
            dst_ref=target,
            send_sem=send,
            recv_sem=receive,
            device_id={axis: index},
            device_id_type=MESH,
        )

    def down(source, halo, send, receive):
        return remote(source, halo.at[1], send.at[1], receive.at[1], "lat", band - 1)

    def up(source, halo, send, receive):
        return remote(source, halo.at[0], send.at[0], receive.at[0], "lat", band + 1)

    def onward(q, source, target, send, receive):
        return remote(
            source.at[q], target.at[q], send.at[q], receive.at[q], "tm", slot + 1
        )

    first = (halo_one, halo_one_s, halo_one_r)
    second = (halo_two, halo_two_s, halo_two_r)
    chain_one = (send_one, recv_one, chain_one_s, chain_one_r)
    chain_two = (send_two, recv_two, chain_two_s, chain_two_r)

    pl.semaphore_wait(
        barrier,
        has_low.astype(jnp.int32) + has_high.astype(jnp.int32) + has_next.astype(jnp.int32),
    )
    pl.when(has_low)(lambda: down(scaled.at[0], *first).start())
    pl.when(has_high)(lambda: up(scaled.at[pairs - 1], *first).start())

    in_pad[...] = jnp.zeros_like(in_pad)
    loads[1].wait()
    loads[2].wait()
    in_pad[0:C, :] = in_t[...].astype(jnp.float32)
    for j in range(HID // W):
        rows = pl.ds(j * W, W)
        in_w[rows, :] = in_pad[:, j * W : (j + 1) * W].T.astype(jnp.bfloat16)
        bias[rows, :] = jnp.broadcast_to(bias_row[:, j * W : (j + 1) * W], (W, W)).T

    half = cond_w.shape[0] // 2
    place = lax.broadcasted_iota(jnp.int32, (1, half), 1).astype(jnp.float32) / half
    frequency = jnp.exp(place * jnp.log(jnp.full((1, half), 100.0, jnp.float32)))
    phases = jnp.log(sigma[:, :1]) / 4.0 * frequency
    embedding = jnp.concatenate([jnp.cos(phases), jnp.sin(phases)], axis=1)
    embedding = jnp.broadcast_to(embedding, (W, 2 * half)).astype(jnp.bfloat16)
    loads[3].wait()
    conditions = jnp.dot(embedding, cond_w[...], preferred_element_type=jnp.float32)
    for j in range(4 * HID // W):
        block = conditions[:, j * W : (j + 1) * W].T
        is_scale = (j * W // HID) % 2 == 0
        cond[pl.ds(j * W, W), :] = block + 1.0 if is_scale else block

    def shifts(target, chunk, halves):
        for i, value in enumerate(halves):
            lanes = pl.ds((2 * chunk + i) * W, W)
            target[pl.ds(0, HID), lanes] = pltpu.roll(value, 1, 1).astype(jnp.bfloat16)
            target[pl.ds(HID, HID), lanes] = value.astype(jnp.bfloat16)
            target[pl.ds(2 * HID, HID), lanes] = pltpu.roll(value, W - 1, 1).astype(jnp.bfloat16)

    def project(chunk, value, inside=None):
        hidden = jnp.dot(in_w[:, :padded], value, preferred_element_type=jnp.float32)
        halves = []
        for i in range(2):
            part = hidden[:, i * W : (i + 1) * W] + bias[...]
            halves.append(part if inside is None else jnp.where(inside, part, 0.0))
        shifts(g_one, chunk, halves)

    def convolve(source, layer, pair):
        rows = [source[:, (2 * pair + a) * W : (2 * pair + a + 2) * W] for a in range(3)]
        return jnp.dot(
            conv_w[layer], jnp.concatenate(rows, axis=0), preferred_element_type=jnp.float32
        )

    def activated(response, layer, i):
        scale = cond[pl.ds(2 * layer * HID, HID), :]
        shift = cond[pl.ds((2 * layer + 1) * HID, HID), :]
        value = response[:, i * W : (i + 1) * W] * scale + shift
        part = 0.5 * value
        return part + part * jnp.tanh(part)

    def after_one(pair, response):
        halves = [activated(response, 0, i) for i in range(2)]
        if pair == 0:
            halves[0] = jnp.where(has_low, halves[0], 0.0)
        if pair == pairs:
            halves[1] = jnp.where(has_high, halves[1], 0.0)
        shifts(g_two, pair, halves)

    def after_two(pair, response, current):
        halves = []
        for i in range(2):
            lanes = pl.ds((2 * pair + 1 + i) * W, W)
            carried = g_two[pl.ds(HID, HID), lanes].astype(jnp.float32)
            halves.append((carried + activated(response, 1, i)).astype(jnp.bfloat16))
        network = jnp.dot(
            out_w[...], jnp.concatenate(halves, axis=1), preferred_element_type=jnp.float32
        )
        drift[pair, 0:C, :] = push * network
        return keep * current + drift[pair]

    def inner(values):
        for q, value in enumerate(values):
            project(q + 1, value)
        responses = [convolve(g_one, 0, pair) for pair in range(1, pairs)]
        for pair, response in enumerate(responses):
            after_one(pair + 1, response)

    def outer(low, high):
        project(0, low, has_low)
        project(pairs + 1, high, has_high)
        responses = [convolve(g_one, 0, pair) for pair in (0, pairs)]
        for pair, response in zip((0, pairs), responses):
            after_one(pair, response)

    def changes(current):
        response = convolve(g_two, 1, 0)
        for q in range(pairs):
            later = convolve(g_two, 1, q + 1) if q + 1 < pairs else None
            yield q, after_two(q, response, current(q))
            response = later

    def write(pair, value):
        for i in range(2):
            result[pl.ds(2 * pair + i, C, stride=R), :] = value[0:C, i * W : (i + 1) * W]

    loads[4].wait()
    inner([scaled[q] for q in range(pairs)])
    loads[5].wait()
    loads[6].wait()
    pl.when(has_low)(lambda: up(scaled.at[pairs - 1], *first).wait_recv())
    pl.when(has_high)(lambda: down(scaled.at[0], *first).wait_recv())
    outer(halo_one[0], halo_one[1])
    for q, change in changes(own):

        @pl.when(slot == 0)
        def _():
            total = own(q) + change
            write(q, total)
            send_one[q] = total.astype(jnp.bfloat16)

        @pl.when(slot > 0)
        def _():
            onward(q, *chain_one).wait_recv()
            if q == 0:
                pl.when(has_low)(lambda: down(recv_one.at[0], *second).start())
            if q == pairs - 1:
                pl.when(has_high)(lambda: up(recv_one.at[pairs - 1], *second).start())
            send_one[q] = (recv_one[q].astype(jnp.float32) + change).astype(jnp.bfloat16)

        pl.when(has_next)(lambda: onward(q, *chain_one).start())

    @pl.when(slot > 0)
    def _():
        def state(q):
            return recv_one[q].astype(jnp.float32)

        def rescaled(value):
            return (value.astype(jnp.float32) * inverse).astype(jnp.bfloat16)

        inner([rescaled(recv_one[q]) for q in range(pairs)])
        pl.when(has_high)(lambda: down(recv_one.at[0], *second).wait_recv())
        pl.when(has_low)(lambda: up(recv_one.at[pairs - 1], *second).wait_recv())
        outer(rescaled(halo_two[0]), rescaled(halo_two[1]))
        for q, change in changes(state):

            @pl.when(slot == 1)
            def _():
                total = state(q) + change
                write(q, total)
                send_two[q] = total.astype(jnp.bfloat16)

            @pl.when(slot > 1)
            def _():
                onward(q, *chain_two).wait_recv()
                total = recv_two[q].astype(jnp.float32) + change
                write(q, total)
                send_two[q] = total.astype(jnp.bfloat16)

            pl.when(has_next)(lambda: onward(q, *chain_two).start())

    pl.when(has_low)(lambda: down(scaled.at[0], *first).wait_send())
    pl.when(has_high)(lambda: up(scaled.at[pairs - 1], *first).wait_send())

    @pl.when(has_next)
    def _():
        for q in range(pairs):
            onward(q, *chain_one).wait_send()

    @pl.when(slot > 0)
    def _():
        pl.when(has_low)(lambda: down(recv_one.at[0], *second).wait_send())
        pl.when(has_high)(lambda: up(recv_one.at[pairs - 1], *second).wait_send())

        @pl.when(has_next)
        def _():
            for q in range(pairs):
                onward(q, *chain_two).wait_send()


def on_device(times, bands, trajectory, step_levels, in_weight, in_bias, conv_weight, cond_weight, out_weight):
    _, C, R, W = trajectory.shape
    HID = in_weight.shape[0]
    pairs = R // 2
    padded = -(-C // 16) * 16
    wide = -(-C // 128) * 128
    bf16, f32 = jnp.bfloat16, jnp.float32
    block = (pairs, padded, 2 * W)
    halo = (2, padded, 2 * W)
    anywhere = pl.BlockSpec(memory_space=pltpu.HBM)
    dma = pltpu.SemaphoreType.DMA
    result = pl.pallas_call(
        functools.partial(kernel, (times, bands, C, R, W, HID)),
        out_shape=jax.ShapeDtypeStruct((C * R, W), f32),
        in_specs=[anywhere] * 7,
        out_specs=pl.BlockSpec(memory_space=pltpu.VMEM),
        scratch_shapes=[
            pltpu.SMEM(step_levels.shape, jnp.int32),
            pltpu.VMEM((padded * R, W), f32),
            pltpu.VMEM((C, HID), bf16),
            pltpu.VMEM((wide, HID), f32),
            pltpu.VMEM((HID, wide), bf16),
            pltpu.VMEM((1, HID), f32),
            pltpu.VMEM(conv_weight.shape, bf16),
            pltpu.VMEM(cond_weight.shape, bf16),
            pltpu.VMEM(out_weight.shape, bf16),
            pltpu.VMEM((4 * HID, W), f32),
            pltpu.VMEM((HID, W), f32),
            pltpu.VMEM((3 * HID, (R + 4) * W), bf16),
            pltpu.VMEM((3 * HID, (R + 2) * W), bf16),
            pltpu.VMEM(block, f32),
            pltpu.VMEM(block, bf16),
            pltpu.VMEM(halo, bf16),
            pltpu.VMEM(block, bf16),
            pltpu.VMEM(block, bf16),
            pltpu.VMEM(halo, bf16),
            pltpu.VMEM(block, bf16),
            pltpu.VMEM(block, bf16),
            dma((8,)),
            dma((2,)),
            dma((2,)),
            dma((pairs,)),
            dma((pairs,)),
            dma((2,)),
            dma((2,)),
            dma((pairs,)),
            dma((pairs,)),
        ],
        compiler_params=pltpu.CompilerParams(
            collective_id=0, has_side_effects=True, vmem_limit_bytes=32 * 1024 * 1024
        ),
    )(
        *(
            pltpu.with_memory_space_constraint(operand, pltpu.HBM)
            for operand in (
                step_levels,
                trajectory.reshape(C * R, W),
                in_weight.T,
                in_bias.reshape(1, HID),
                conv_weight,
                cond_weight,
                out_weight,
            )
        ),
    )
    return result.reshape(1, C, R, W)


def solution(mesh):
    in_specs = (P("tm", None, "lat", None), P(), P(), P(), P(), P(), P())
    out_specs = P("tm", None, "lat", None)
    return jax.shard_map(
        functools.partial(on_device, mesh.shape["tm"], mesh.shape["lat"]),
        mesh=mesh,
        in_specs=in_specs,
        out_specs=out_specs,
        check_vma=False,
    )
```

```python
import functools

import jax
import jax.numpy as jnp
from jax import lax
from jax.experimental import pallas as pl
from jax.experimental.pallas import tpu as pltpu
from jax.sharding import PartitionSpec as P

LEVELS = 64
MESH = pl.DeviceIdType.MESH

sigma_top = 1.0
sigma_low = 0.02
rho_power = 7.0


def level_sigma(level):
    top, low = sigma_top ** (1.0 / rho_power), sigma_low ** (1.0 / rho_power)
    root = top + level.astype(jnp.float32) / (LEVELS - 1) * (low - top)
    square = root * root
    return square * square * square * root


def kernel(
    sizes,
    levels_hbm,
    x_hbm,
    in_hbm,
    bias_hbm,
    conv_hbm,
    cond_hbm,
    out_hbm,
    result,
    levels,
    xs,
    in_t,
    in_pad,
    in_w,
    bias_row,
    conv_w,
    cond_w,
    out_w,
    cond,
    bias,
    g_one,
    g_two,
    drift,
    scaled,
    halo_one,
    recv_one,
    send_one,
    halo_two,
    recv_two,
    send_two,
    load_sem,
    halo_one_s,
    halo_one_r,
    chain_one_s,
    chain_one_r,
    halo_two_s,
    halo_two_r,
    chain_two_s,
    chain_two_r,
):
    times, bands, C, R, W, HID = sizes
    pairs = R // 2
    W2 = 2 * W
    padded = scaled.shape[1]
    slot = lax.axis_index("tm")
    band = lax.axis_index("lat")
    has_low, has_high = band > 0, band < bands - 1
    has_next = slot < times - 1

    loads = [
        pltpu.make_async_copy(source, target, load_sem.at[i])
        for i, (source, target) in enumerate(
            [
                (x_hbm, xs.at[pl.ds(0, C * R)]),
                (in_hbm, in_t),
                (bias_hbm, bias_row),
                (cond_hbm, cond_w),
                (conv_hbm.at[0], conv_w.at[0]),
                (conv_hbm.at[1], conv_w.at[1]),
                (out_hbm, out_w),
                (levels_hbm, levels),
            ]
        )
    ]
    for load in loads[-1:] + loads[:-1]:
        load.start()

    barrier = pltpu.get_barrier_semaphore()

    def greet(axis, index):
        pl.semaphore_signal(barrier, inc=1, device_id={axis: index}, device_id_type=MESH)

    pl.when(has_low)(lambda: greet("lat", band - 1))
    pl.when(has_high)(lambda: greet("lat", band + 1))
    pl.when(slot > 0)(lambda: greet("tm", slot - 1))

    if padded > C:
        xs[C * R :, :] = jnp.zeros((padded * R - C * R, W), jnp.float32)
    drift[...] = jnp.zeros_like(drift)

    loads[7].wait()
    sigma = level_sigma(jnp.full((1, W2), levels[slot], jnp.int32))
    sigma_next = level_sigma(jnp.full((1, W2), levels[slot + 1], jnp.int32))
    variance = sigma * sigma + 0.25
    inverse = 1.0 / jnp.sqrt(variance)
    gain = (sigma_next - sigma) / sigma
    keep = gain * (sigma * sigma / variance)
    push = -0.5 * gain * sigma * inverse

    def own(q):
        return jnp.concatenate(
            [xs[pl.ds(2 * q + i, padded, stride=R), :] for i in range(2)], axis=1
        )

    loads[0].wait()
    for q in range(pairs):
        scaled[q] = (own(q) * inverse).astype(jnp.bfloat16)

    def remote(source, target, send, receive, axis, index):
        return pltpu.make_async_remote_copy(
            src_ref=source,
            dst_ref=target,
            send_sem=send,
            recv_sem=receive,
            device_id={axis: index},
            device_id_type=MESH,
        )

    def down(source, halo, send, receive):
        return remote(source, halo.at[1], send.at[1], receive.at[1], "lat", band - 1)

    def up(source, halo, send, receive):
        return remote(source, halo.at[0], send.at[0], receive.at[0], "lat", band + 1)

    def onward(q, source, target, send, receive):
        return remote(
            source.at[q], target.at[q], send.at[q], receive.at[q], "tm", slot + 1
        )

    first = (halo_one, halo_one_s, halo_one_r)
    second = (halo_two, halo_two_s, halo_two_r)
    chain_one = (send_one, recv_one, chain_one_s, chain_one_r)
    chain_two = (send_two, recv_two, chain_two_s, chain_two_r)

    pl.semaphore_wait(
        barrier,
        has_low.astype(jnp.int32) + has_high.astype(jnp.int32) + has_next.astype(jnp.int32),
    )
    pl.when(has_low)(lambda: down(scaled.at[0], *first).start())
    pl.when(has_high)(lambda: up(scaled.at[pairs - 1], *first).start())

    in_pad[...] = jnp.zeros_like(in_pad)
    loads[1].wait()
    loads[2].wait()
    in_pad[0:C, :] = in_t[...].astype(jnp.float32)
    for j in range(HID // W):
        rows = pl.ds(j * W, W)
        in_w[rows, :] = in_pad[:, j * W : (j + 1) * W].T.astype(jnp.bfloat16)
        bias[rows, :] = jnp.broadcast_to(bias_row[:, j * W : (j + 1) * W], (W, W)).T

    half = cond_w.shape[0] // 2
    place = lax.broadcasted_iota(jnp.int32, (1, half), 1).astype(jnp.float32) / half
    frequency = jnp.exp(place * jnp.log(jnp.full((1, half), 100.0, jnp.float32)))
    phases = jnp.log(sigma[:, :1]) / 4.0 * frequency
    embedding = jnp.concatenate([jnp.cos(phases), jnp.sin(phases)], axis=1)
    embedding = jnp.broadcast_to(embedding, (W, 2 * half)).astype(jnp.bfloat16)
    loads[3].wait()
    conditions = jnp.dot(embedding, cond_w[...], preferred_element_type=jnp.float32)
    for j in range(4 * HID // W):
        block = conditions[:, j * W : (j + 1) * W].T
        is_scale = (j * W // HID) % 2 == 0
        cond[pl.ds(j * W, W), :] = block + 1.0 if is_scale else block

    def shifts(target, chunk, halves):
        for i, half in enumerate(halves):
            lanes = pl.ds((2 * chunk + i) * W, W)
            value = half.astype(jnp.bfloat16)
            target[pl.ds(0, HID), lanes] = pltpu.roll(value, 1, 1)
            target[pl.ds(HID, HID), lanes] = value
            target[pl.ds(2 * HID, HID), lanes] = pltpu.roll(value, W - 1, 1)

    def project(chunks, values, insides=None):
        hidden = jnp.dot(
            in_w[:, :padded],
            jnp.concatenate(values, axis=1),
            preferred_element_type=jnp.float32,
        )
        for j, chunk in enumerate(chunks):
            halves = []
            for i in range(2):
                part = hidden[:, (2 * j + i) * W : (2 * j + i + 1) * W] + bias[...]
                halves.append(part if insides is None else jnp.where(insides[j], part, 0.0))
            shifts(g_one, chunk, halves)

    def convolve(source, layer, firsts):
        rows = [
            jnp.concatenate(
                [source[:, (2 * pair + a) * W : (2 * pair + a + 2) * W] for pair in firsts], axis=1
            )
            for a in range(3)
        ]
        response = jnp.dot(
            conv_w[layer], jnp.concatenate(rows, axis=0), preferred_element_type=jnp.float32
        )
        return [response[:, j * W2 : (j + 1) * W2] for j in range(len(firsts))]

    def activated(response, layer, i):
        scale = cond[pl.ds(2 * layer * HID, HID), :]
        shift = cond[pl.ds((2 * layer + 1) * HID, HID), :]
        value = response[:, i * W : (i + 1) * W] * scale + shift
        part = 0.5 * value
        return part + part * jnp.tanh(part)

    def after_one(pair, response):
        halves = [activated(response, 0, i) for i in range(2)]
        if pair == 0:
            halves[0] = jnp.where(has_low, halves[0], 0.0)
        if pair == pairs:
            halves[1] = jnp.where(has_high, halves[1], 0.0)
        shifts(g_two, pair, halves)

    def inner(values):
        project(range(1, pairs + 1), values)
        middle = range(1, pairs)
        if middle:
            for pair, response in zip(middle, convolve(g_one, 0, middle)):
                after_one(pair, response)

    def outer(low, high):
        project((0, pairs + 1), (low, high), (has_low, has_high))
        for pair, response in zip((0, pairs), convolve(g_one, 0, (0, pairs))):
            after_one(pair, response)

    def changes(current):
        halves = []
        for q, response in enumerate(convolve(g_two, 1, range(pairs))):
            for i in range(2):
                lanes = pl.ds((2 * q + 1 + i) * W, W)
                carried = g_two[pl.ds(HID, HID), lanes].astype(jnp.float32)
                halves.append((carried + activated(response, 1, i)).astype(jnp.bfloat16))
        network = jnp.dot(
            out_w[...], jnp.concatenate(halves, axis=1), preferred_element_type=jnp.float32
        )
        for q in range(pairs):
            drift[q, 0:C, :] = push * network[:, q * W2 : (q + 1) * W2]
        for q in range(pairs):
            yield q, keep * current(q) + drift[q]

    def write(pair, value):
        for i in range(2):
            result[pl.ds(2 * pair + i, C, stride=R), :] = value[0:C, i * W : (i + 1) * W]

    loads[4].wait()
    inner([scaled[q] for q in range(pairs)])
    loads[5].wait()
    loads[6].wait()
    pl.when(has_low)(lambda: up(scaled.at[pairs - 1], *first).wait_recv())
    pl.when(has_high)(lambda: down(scaled.at[0], *first).wait_recv())
    outer(halo_one[0], halo_one[1])
    for q, change in changes(own):

        @pl.when(slot == 0)
        def _():
            total = own(q) + change
            write(q, total)
            send_one[q] = total.astype(jnp.bfloat16)

        @pl.when(slot > 0)
        def _():
            onward(q, *chain_one).wait_recv()
            if q == 0:
                pl.when(has_low)(lambda: down(recv_one.at[0], *second).start())
            if q == pairs - 1:
                pl.when(has_high)(lambda: up(recv_one.at[pairs - 1], *second).start())
            send_one[q] = (recv_one[q].astype(jnp.float32) + change).astype(jnp.bfloat16)

        pl.when(has_next)(lambda: onward(q, *chain_one).start())

    @pl.when(slot > 0)
    def _():
        def state(q):
            return recv_one[q].astype(jnp.float32)

        def rescaled(value):
            return (value.astype(jnp.float32) * inverse).astype(jnp.bfloat16)

        inner([rescaled(recv_one[q]) for q in range(pairs)])
        pl.when(has_high)(lambda: down(recv_one.at[0], *second).wait_recv())
        pl.when(has_low)(lambda: up(recv_one.at[pairs - 1], *second).wait_recv())
        outer(rescaled(halo_two[0]), rescaled(halo_two[1]))
        for q, change in changes(state):

            @pl.when(slot == 1)
            def _():
                total = state(q) + change
                write(q, total)
                send_two[q] = total.astype(jnp.bfloat16)

            @pl.when(slot > 1)
            def _():
                onward(q, *chain_two).wait_recv()
                total = recv_two[q].astype(jnp.float32) + change
                write(q, total)
                send_two[q] = total.astype(jnp.bfloat16)

            pl.when(has_next)(lambda: onward(q, *chain_two).start())

    pl.when(has_low)(lambda: down(scaled.at[0], *first).wait_send())
    pl.when(has_high)(lambda: up(scaled.at[pairs - 1], *first).wait_send())

    @pl.when(has_next)
    def _():
        for q in range(pairs):
            onward(q, *chain_one).wait_send()

    @pl.when(slot > 0)
    def _():
        pl.when(has_low)(lambda: down(recv_one.at[0], *second).wait_send())
        pl.when(has_high)(lambda: up(recv_one.at[pairs - 1], *second).wait_send())

        @pl.when(has_next)
        def _():
            for q in range(pairs):
                onward(q, *chain_two).wait_send()


def on_device(times, bands, trajectory, step_levels, in_weight, in_bias, conv_weight, cond_weight, out_weight):
    _, C, R, W = trajectory.shape
    HID = in_weight.shape[0]
    pairs = R // 2
    padded = -(-C // 16) * 16
    wide = -(-C // 128) * 128
    bf16, f32 = jnp.bfloat16, jnp.float32
    block = (pairs, padded, 2 * W)
    halo = (2, padded, 2 * W)
    anywhere = pl.BlockSpec(memory_space=pltpu.HBM)
    dma = pltpu.SemaphoreType.DMA
    result = pl.pallas_call(
        functools.partial(kernel, (times, bands, C, R, W, HID)),
        out_shape=jax.ShapeDtypeStruct((C * R, W), f32),
        in_specs=[anywhere] * 7,
        out_specs=pl.BlockSpec(memory_space=pltpu.VMEM),
        scratch_shapes=[
            pltpu.SMEM(step_levels.shape, jnp.int32),
            pltpu.VMEM((padded * R, W), f32),
            pltpu.VMEM((C, HID), bf16),
            pltpu.VMEM((wide, HID), f32),
            pltpu.VMEM((HID, wide), bf16),
            pltpu.VMEM((1, HID), f32),
            pltpu.VMEM(conv_weight.shape, bf16),
            pltpu.VMEM(cond_weight.shape, bf16),
            pltpu.VMEM(out_weight.shape, bf16),
            pltpu.VMEM((4 * HID, W), f32),
            pltpu.VMEM((HID, W), f32),
            pltpu.VMEM((3 * HID, (R + 4) * W), bf16),
            pltpu.VMEM((3 * HID, (R + 2) * W), bf16),
            pltpu.VMEM(block, f32),
            pltpu.VMEM(block, bf16),
            pltpu.VMEM(halo, bf16),
            pltpu.VMEM(block, bf16),
            pltpu.VMEM(block, bf16),
            pltpu.VMEM(halo, bf16),
            pltpu.VMEM(block, bf16),
            pltpu.VMEM(block, bf16),
            dma((8,)),
            dma((2,)),
            dma((2,)),
            dma((pairs,)),
            dma((pairs,)),
            dma((2,)),
            dma((2,)),
            dma((pairs,)),
            dma((pairs,)),
        ],
        compiler_params=pltpu.CompilerParams(
            collective_id=0, has_side_effects=True, vmem_limit_bytes=32 * 1024 * 1024
        ),
    )(
        *(
            pltpu.with_memory_space_constraint(operand, pltpu.HBM)
            for operand in (
                step_levels,
                trajectory.reshape(C * R, W),
                in_weight.T,
                in_bias.reshape(1, HID),
                conv_weight,
                cond_weight,
                out_weight,
            )
        ),
    )
    return result.reshape(1, C, R, W)


def solution(mesh):
    in_specs = (P("tm", None, "lat", None), P(), P(), P(), P(), P(), P())
    out_specs = P("tm", None, "lat", None)
    return jax.shard_map(
        functools.partial(on_device, mesh.shape["tm"], mesh.shape["lat"]),
        mesh=mesh,
        in_specs=in_specs,
        out_specs=out_specs,
        check_vma=False,
    )
```

```python
import functools

import jax
import jax.numpy as jnp
from jax import lax
from jax.experimental import pallas as pl
from jax.experimental.pallas import tpu as pltpu
from jax.sharding import PartitionSpec as P

LEVELS = 64
MESH = pl.DeviceIdType.MESH

sigma_top = 1.0
sigma_low = 0.02
rho_power = 7.0


def level_sigma(level):
    top, low = sigma_top ** (1.0 / rho_power), sigma_low ** (1.0 / rho_power)
    root = top + level.astype(jnp.float32) / (LEVELS - 1) * (low - top)
    square = root * root
    return square * square * square * root


def kernel(
    sizes,
    levels_hbm,
    x_hbm,
    in_hbm,
    bias_hbm,
    conv_hbm,
    cond_hbm,
    out_hbm,
    result,
    levels,
    xs,
    in_t,
    in_pad,
    in_w,
    bias_row,
    conv_w,
    cond_w,
    out_w,
    cond,
    bias,
    g_one,
    g_two,
    state,
    drift,
    scaled,
    halo,
    recv,
    send,
    load_sem,
    halo_s,
    halo_r,
    chain_s,
    chain_r,
    ready,
):
    times, bands, C, R, W, HID = sizes
    pairs = R // 2
    W2 = 2 * W
    padded = scaled.shape[2]
    slot = lax.axis_index("tm")
    band = lax.axis_index("lat")
    has_low, has_high = band > 0, band < bands - 1
    has_next = slot < times - 1

    barrier = pltpu.get_barrier_semaphore()

    def greet(axis, index):
        pl.semaphore_signal(barrier, inc=1, device_id={axis: index}, device_id_type=MESH)

    pl.when(has_low)(lambda: greet("lat", band - 1))
    pl.when(has_high)(lambda: greet("lat", band + 1))
    pl.when(has_next)(lambda: greet("tm", slot + 1))

    loads = [
        pltpu.make_async_copy(source, target, load_sem.at[i])
        for i, (source, target) in enumerate(
            [
                (x_hbm, xs.at[pl.ds(0, C * R)]),
                (in_hbm, in_t),
                (bias_hbm, bias_row),
                (cond_hbm, cond_w),
                (conv_hbm.at[0], conv_w.at[0]),
                (conv_hbm.at[1], conv_w.at[1]),
                (out_hbm, out_w),
                (levels_hbm, levels),
            ]
        )
    ]
    for load in loads[-1:] + loads[:-1]:
        load.start()

    if padded > C:
        xs[C * R :, :] = jnp.zeros((padded * R - C * R, W), jnp.float32)
    drift[...] = jnp.zeros_like(drift)

    loads[7].wait()
    sigma = level_sigma(jnp.full((1, W2), levels[slot], jnp.int32))
    sigma_next = level_sigma(jnp.full((1, W2), levels[slot + 1], jnp.int32))
    variance = sigma * sigma + 0.25
    inverse = 1.0 / jnp.sqrt(variance)
    gain = (sigma_next - sigma) / sigma
    keep = gain * (sigma * sigma / variance)
    push = -0.5 * gain * sigma * inverse

    def own(q):
        return jnp.concatenate(
            [xs[pl.ds(2 * q + i, padded, stride=R), :] for i in range(2)], axis=1
        )

    loads[0].wait()
    for q in range(pairs):
        value = own(q)
        state[q] = value
        scaled[0, q] = (value * inverse).astype(jnp.bfloat16)

    def remote(source, target, send_sem, recv_sem, axis, index):
        return pltpu.make_async_remote_copy(
            src_ref=source,
            dst_ref=target,
            send_sem=send_sem,
            recv_sem=recv_sem,
            device_id={axis: index},
            device_id_type=MESH,
        )

    def down(source, s):
        return remote(source, halo.at[s, 1], halo_s.at[s, 1], halo_r.at[s, 1], "lat", band - 1)

    def up(source, s):
        return remote(source, halo.at[s, 0], halo_s.at[s, 0], halo_r.at[s, 0], "lat", band + 1)

    def onward(s, q):
        return remote(
            send.at[s, q], recv.at[s, q], chain_s.at[s, q], chain_r.at[s, q], "tm", slot + 1
        )

    pl.semaphore_wait(
        barrier,
        has_low.astype(jnp.int32) + has_high.astype(jnp.int32) + (slot > 0).astype(jnp.int32),
    )
    pl.when(has_low)(lambda: down(scaled.at[0, 0], 0).start())
    pl.when(has_high)(lambda: up(scaled.at[0, pairs - 1], 0).start())

    @pl.when(slot > 0)
    def _():
        pl.semaphore_signal(ready, inc=1, device_id={"tm": slot - 1}, device_id_type=MESH)

    in_pad[...] = jnp.zeros_like(in_pad)
    loads[1].wait()
    loads[2].wait()
    in_pad[0:C, :] = in_t[...].astype(jnp.float32)
    for j in range(HID // W):
        rows = pl.ds(j * W, W)
        in_w[rows, :] = in_pad[:, j * W : (j + 1) * W].T.astype(jnp.bfloat16)
        bias[rows, :] = jnp.broadcast_to(bias_row[:, j * W : (j + 1) * W], (W, W)).T

    half = cond_w.shape[0] // 2
    place = lax.broadcasted_iota(jnp.int32, (1, half), 1).astype(jnp.float32) / half
    frequency = jnp.exp(place * jnp.log(jnp.full((1, half), 100.0, jnp.float32)))
    phases = jnp.log(sigma[:, :1]) / 4.0 * frequency
    embedding = jnp.concatenate([jnp.cos(phases), jnp.sin(phases)], axis=1)
    embedding = jnp.broadcast_to(embedding, (W, 2 * half)).astype(jnp.bfloat16)
    loads[3].wait()
    conditions = jnp.dot(embedding, cond_w[...], preferred_element_type=jnp.float32)
    for j in range(4 * HID // W):
        block = conditions[:, j * W : (j + 1) * W].T
        is_scale = (j * W // HID) % 2 == 0
        cond[pl.ds(j * W, W), :] = block + 1.0 if is_scale else block

    def lanes(row, count):
        return pl.ds(pl.multiple_of(row * W, W), count * W)

    def shifts(target, chunk, halves):
        for i, half in enumerate(halves):
            value = half.astype(jnp.bfloat16)
            place = lanes(2 * chunk + i, 1)
            target[pl.ds(0, HID), place] = pltpu.roll(value, 1, 1)
            target[pl.ds(HID, HID), place] = value
            target[pl.ds(2 * HID, HID), place] = pltpu.roll(value, W - 1, 1)

    def project(chunks, values, insides=None):
        hidden = jnp.dot(
            in_w[:, :padded],
            jnp.concatenate(values, axis=1),
            preferred_element_type=jnp.float32,
        )
        for j, chunk in enumerate(chunks):
            halves = []
            for i in range(2):
                part = hidden[:, (2 * j + i) * W : (2 * j + i + 1) * W] + bias[...]
                halves.append(part if insides is None else jnp.where(insides[j], part, 0.0))
            shifts(g_one, chunk, halves)

    def convolve(source, layer, pair):
        rows = [source[:, lanes(2 * pair + a, 2)] for a in range(3)]
        return jnp.dot(
            conv_w[layer], jnp.concatenate(rows, axis=0), preferred_element_type=jnp.float32
        )

    def activated(response, layer, i):
        scale = cond[pl.ds(2 * layer * HID, HID), :]
        shift = cond[pl.ds((2 * layer + 1) * HID, HID), :]
        value = response[:, i * W : (i + 1) * W] * scale + shift
        part = 0.5 * value
        return part + part * jnp.tanh(part)

    def write(pair, value):
        for i in range(2):
            result[pl.ds(2 * pair + i, C, stride=R), :] = value[0:C, i * W : (i + 1) * W]

    loads[4].wait()
    loads[5].wait()
    loads[6].wait()
    pl.when(has_next)(lambda: pl.semaphore_wait(ready, 1))

    def sweep(s, _):
        @pl.when(s > 0)
        def _():
            for q in range(pairs):
                value = recv[0, q].astype(jnp.float32)
                state[q] = value
                scaled[1, q] = (value * inverse).astype(jnp.bfloat16)

        project(range(1, pairs + 1), [scaled[s, q] for q in range(pairs)])

        def layer_one(t, _):
            @pl.when(t == pairs - 1)
            def _():
                pl.when(has_low)(lambda: up(scaled.at[0, pairs - 1], s).wait_recv())
                pl.when(has_high)(lambda: down(scaled.at[0, 0], s).wait_recv())
                factor = jnp.where(jnp.full((1, W2), s, jnp.int32) > 0, inverse, 1.0)
                values = [
                    (halo[s, i].astype(jnp.float32) * factor).astype(jnp.bfloat16) for i in range(2)
                ]
                project((0, pairs + 1), values, (has_low, has_high))

            pair = jnp.where(t < pairs - 1, t + 1, jnp.where(t == pairs, pairs, 0))
            response = convolve(g_one, 0, pair)
            insides = (jnp.logical_or(pair > 0, has_low), jnp.logical_or(pair < pairs, has_high))
            halves = [jnp.where(insides[i], activated(response, 0, i), 0.0) for i in range(2)]
            shifts(g_two, pair, halves)
            return 0

        lax.fori_loop(0, pairs + 1, layer_one, 0)

        def layer_two(q, _):
            response = convolve(g_two, 1, q)
            halves = []
            for i in range(2):
                carried = g_two[pl.ds(HID, HID), lanes(2 * q + 1 + i, 1)].astype(jnp.float32)
                halves.append((carried + activated(response, 1, i)).astype(jnp.bfloat16))
            network = jnp.dot(
                out_w[...], jnp.concatenate(halves, axis=1), preferred_element_type=jnp.float32
            )
            drift[q, 0:C, :] = push * network
            return 0

        lax.fori_loop(0, pairs, layer_two, 0)

        for q in range(pairs):

            @pl.when(slot > s)
            def _():
                onward(s, q).wait_recv()

                @pl.when(s == 0)
                def _():
                    if q == 0:
                        pl.when(has_low)(lambda: down(recv.at[0, 0], 1).start())
                    if q == pairs - 1:
                        pl.when(has_high)(lambda: up(recv.at[0, pairs - 1], 1).start())

            change = keep * state[q] + drift[q]
            base = jnp.where(slot == s, state[q], recv[s, q].astype(jnp.float32))
            total = base + change
            send[s, q] = total.astype(jnp.bfloat16)
            pl.when(has_next)(lambda: onward(s, q).start())

            @pl.when(jnp.logical_or(s > 0, slot == 0))
            def _():
                write(q, total)

        return 0

    lax.fori_loop(0, jnp.where(slot > 0, 2, 1), sweep, 0)

    for s in range(2):

        @pl.when(slot >= s)
        def _():
            first, last = (scaled.at[0, 0], scaled.at[0, pairs - 1]) if s == 0 else (
                recv.at[0, 0],
                recv.at[0, pairs - 1],
            )
            pl.when(has_low)(lambda: down(first, s).wait_send())
            pl.when(has_high)(lambda: up(last, s).wait_send())

            @pl.when(has_next)
            def _():
                for q in range(pairs):
                    onward(s, q).wait_send()


def on_device(times, bands, trajectory, step_levels, in_weight, in_bias, conv_weight, cond_weight, out_weight):
    _, C, R, W = trajectory.shape
    HID = in_weight.shape[0]
    pairs = R // 2
    padded = -(-C // 16) * 16
    wide = -(-C // 128) * 128
    bf16, f32 = jnp.bfloat16, jnp.float32
    block = (pairs, padded, 2 * W)
    halo = (2, padded, 2 * W)
    anywhere = pl.BlockSpec(memory_space=pltpu.HBM)
    dma = pltpu.SemaphoreType.DMA
    result = pl.pallas_call(
        functools.partial(kernel, (times, bands, C, R, W, HID)),
        out_shape=jax.ShapeDtypeStruct((C * R, W), f32),
        in_specs=[anywhere] * 7,
        out_specs=pl.BlockSpec(memory_space=pltpu.VMEM),
        scratch_shapes=[
            pltpu.SMEM(step_levels.shape, jnp.int32),
            pltpu.VMEM((padded * R, W), f32),
            pltpu.VMEM((C, HID), bf16),
            pltpu.VMEM((wide, HID), f32),
            pltpu.VMEM((HID, wide), bf16),
            pltpu.VMEM((1, HID), f32),
            pltpu.VMEM(conv_weight.shape, bf16),
            pltpu.VMEM(cond_weight.shape, bf16),
            pltpu.VMEM(out_weight.shape, bf16),
            pltpu.VMEM((4 * HID, W), f32),
            pltpu.VMEM((HID, W), f32),
            pltpu.VMEM((3 * HID, (R + 4) * W), bf16),
            pltpu.VMEM((3 * HID, (R + 2) * W), bf16),
            pltpu.VMEM(block, f32),
            pltpu.VMEM(block, f32),
            pltpu.VMEM((2,) + block, bf16),
            pltpu.VMEM((2,) + halo, bf16),
            pltpu.VMEM((2,) + block, bf16),
            pltpu.VMEM((2,) + block, bf16),
            dma((8,)),
            dma((2, 2)),
            dma((2, 2)),
            dma((2, pairs)),
            dma((2, pairs)),
            pltpu.SemaphoreType.REGULAR,
        ],
        compiler_params=pltpu.CompilerParams(
            collective_id=0, has_side_effects=True, vmem_limit_bytes=32 * 1024 * 1024
        ),
    )(
        *(
            pltpu.with_memory_space_constraint(operand, pltpu.HBM)
            for operand in (
                step_levels,
                trajectory.reshape(C * R, W),
                in_weight.T,
                in_bias.reshape(1, HID),
                conv_weight,
                cond_weight,
                out_weight,
            )
        ),
    )
    return result.reshape(1, C, R, W)


def solution(mesh):
    in_specs = (P("tm", None, "lat", None), P(), P(), P(), P(), P(), P())
    out_specs = P("tm", None, "lat", None)
    return jax.shard_map(
        functools.partial(on_device, mesh.shape["tm"], mesh.shape["lat"]),
        mesh=mesh,
        in_specs=in_specs,
        out_specs=out_specs,
        check_vma=False,
    )
```

```python
import functools

import jax
import jax.numpy as jnp
from jax import lax
from jax.experimental import pallas as pl
from jax.experimental.pallas import tpu as pltpu
from jax.sharding import PartitionSpec as P

LEVELS = 64
MESH = pl.DeviceIdType.MESH

sigma_top = 1.0
sigma_low = 0.02
rho_power = 7.0


def level_sigma(level):
    top, low = sigma_top ** (1.0 / rho_power), sigma_low ** (1.0 / rho_power)
    root = top + level.astype(jnp.float32) / (LEVELS - 1) * (low - top)
    square = root * root
    return square * square * square * root


def kernel(
    sizes,
    levels_hbm,
    x_hbm,
    in_hbm,
    bias_hbm,
    conv_hbm,
    cond_hbm,
    out_hbm,
    result,
    levels,
    xs,
    in_t,
    in_pad,
    in_w,
    bias_row,
    conv_w,
    cond_w,
    out_w,
    cond,
    bias,
    g_one,
    g_two,
    drift,
    scaled,
    halo_one,
    recv_one,
    send_one,
    halo_two,
    recv_two,
    send_two,
    load_sem,
    halo_one_s,
    halo_one_r,
    chain_one_s,
    chain_one_r,
    halo_two_s,
    halo_two_r,
    chain_two_s,
    chain_two_r,
    ready,
):
    times, bands, C, R, W, HID = sizes
    pairs = R // 2
    W2 = 2 * W
    padded = scaled.shape[1]
    slot = lax.axis_index("tm")
    band = lax.axis_index("lat")
    has_low, has_high = band > 0, band < bands - 1
    has_next = slot < times - 1

    barrier = pltpu.get_barrier_semaphore()

    def greet(axis, index):
        pl.semaphore_signal(barrier, inc=1, device_id={axis: index}, device_id_type=MESH)

    pl.when(has_low)(lambda: greet("lat", band - 1))
    pl.when(has_high)(lambda: greet("lat", band + 1))
    pl.when(has_next)(lambda: greet("tm", slot + 1))

    loads = [
        pltpu.make_async_copy(source, target, load_sem.at[i])
        for i, (source, target) in enumerate(
            [
                (x_hbm, xs.at[pl.ds(0, C * R)]),
                (in_hbm, in_t),
                (bias_hbm, bias_row),
                (cond_hbm, cond_w),
                (conv_hbm.at[0], conv_w.at[0]),
                (conv_hbm.at[1], conv_w.at[1]),
                (out_hbm, out_w),
                (levels_hbm, levels),
            ]
        )
    ]
    for load in loads[-1:] + loads[:-1]:
        load.start()

    if padded > C:
        xs[C * R :, :] = jnp.zeros((padded * R - C * R, W), jnp.float32)
    drift[...] = jnp.zeros_like(drift)

    loads[7].wait()
    sigma = level_sigma(jnp.full((1, W2), levels[slot], jnp.int32))
    sigma_next = level_sigma(jnp.full((1, W2), levels[slot + 1], jnp.int32))
    variance = sigma * sigma + 0.25
    inverse = 1.0 / jnp.sqrt(variance)
    gain = (sigma_next - sigma) / sigma
    keep = gain * (sigma * sigma / variance)
    push = -0.5 * gain * sigma * inverse

    def own(q):
        return jnp.concatenate(
            [xs[pl.ds(2 * q + i, padded, stride=R), :] for i in range(2)], axis=1
        )

    loads[0].wait()
    for q in range(pairs):
        scaled[q] = (own(q) * inverse).astype(jnp.bfloat16)

    def remote(source, target, send, receive, axis, index):
        return pltpu.make_async_remote_copy(
            src_ref=source,
            dst_ref=target,
            send_sem=send,
            recv_sem=receive,
            device_id={axis: index},
            device_id_type=MESH,
        )

    def down(source, halo, send, receive):
        return remote(source, halo.at[1], send.at[1], receive.at[1], "lat", band - 1)

    def up(source, halo, send, receive):
        return remote(source, halo.at[0], send.at[0], receive.at[0], "lat", band + 1)

    def onward(q, source, target, send, receive):
        return remote(
            source.at[q], target.at[q], send.at[q], receive.at[q], "tm", slot + 1
        )

    first = (halo_one, halo_one_s, halo_one_r)
    second = (halo_two, halo_two_s, halo_two_r)
    chain_one = (send_one, recv_one, chain_one_s, chain_one_r)
    chain_two = (send_two, recv_two, chain_two_s, chain_two_r)

    pl.semaphore_wait(
        barrier,
        has_low.astype(jnp.int32) + has_high.astype(jnp.int32) + (slot > 0).astype(jnp.int32),
    )
    pl.when(has_low)(lambda: down(scaled.at[0], *first).start())
    pl.when(has_high)(lambda: up(scaled.at[pairs - 1], *first).start())

    @pl.when(slot > 0)
    def _():
        pl.semaphore_signal(ready, inc=1, device_id={"tm": slot - 1}, device_id_type=MESH)


    in_pad[...] = jnp.zeros_like(in_pad)
    loads[1].wait()
    loads[2].wait()
    in_pad[0:C, :] = in_t[...].astype(jnp.float32)
    for j in range(HID // W):
        rows = pl.ds(j * W, W)
        in_w[rows, :] = in_pad[:, j * W : (j + 1) * W].T.astype(jnp.bfloat16)
        bias[rows, :] = jnp.broadcast_to(bias_row[:, j * W : (j + 1) * W], (W, W)).T

    half = cond_w.shape[0] // 2
    place = lax.broadcasted_iota(jnp.int32, (1, half), 1).astype(jnp.float32) / half
    frequency = jnp.exp(place * jnp.log(jnp.full((1, half), 100.0, jnp.float32)))
    phases = jnp.log(sigma[:, :1]) / 4.0 * frequency
    embedding = jnp.concatenate([jnp.cos(phases), jnp.sin(phases)], axis=1)
    embedding = jnp.broadcast_to(embedding, (W, 2 * half)).astype(jnp.bfloat16)
    loads[3].wait()
    conditions = jnp.dot(embedding, cond_w[...], preferred_element_type=jnp.float32)
    for j in range(4 * HID // W):
        block = conditions[:, j * W : (j + 1) * W].T
        is_scale = (j * W // HID) % 2 == 0
        cond[pl.ds(j * W, W), :] = block + 1.0 if is_scale else block

    def shifts(target, chunk, halves):
        for i, half in enumerate(halves):
            lanes = pl.ds((2 * chunk + i) * W, W)
            value = half.astype(jnp.bfloat16)
            target[pl.ds(0, HID), lanes] = pltpu.roll(value, 1, 1)
            target[pl.ds(HID, HID), lanes] = value
            target[pl.ds(2 * HID, HID), lanes] = pltpu.roll(value, W - 1, 1)

    def project(chunks, values, insides=None):
        hidden = jnp.dot(
            in_w[:, :padded],
            jnp.concatenate(values, axis=1),
            preferred_element_type=jnp.float32,
        )
        for j, chunk in enumerate(chunks):
            halves = []
            for i in range(2):
                part = hidden[:, (2 * j + i) * W : (2 * j + i + 1) * W] + bias[...]
                halves.append(part if insides is None else jnp.where(insides[j], part, 0.0))
            shifts(g_one, chunk, halves)

    def convolve(source, layer, firsts):
        rows = [
            jnp.concatenate(
                [source[:, (2 * pair + a) * W : (2 * pair + a + 2) * W] for pair in firsts], axis=1
            )
            for a in range(3)
        ]
        response = jnp.dot(
            conv_w[layer], jnp.concatenate(rows, axis=0), preferred_element_type=jnp.float32
        )
        return [response[:, j * W2 : (j + 1) * W2] for j in range(len(firsts))]

    def activated(response, layer, i):
        scale = cond[pl.ds(2 * layer * HID, HID), :]
        shift = cond[pl.ds((2 * layer + 1) * HID, HID), :]
        value = response[:, i * W : (i + 1) * W] * scale + shift
        part = 0.5 * value
        return part + part * jnp.tanh(part)

    def after_one(pair, response):
        halves = [activated(response, 0, i) for i in range(2)]
        if pair == 0:
            halves[0] = jnp.where(has_low, halves[0], 0.0)
        if pair == pairs:
            halves[1] = jnp.where(has_high, halves[1], 0.0)
        shifts(g_two, pair, halves)

    def inner(values):
        project(range(1, pairs + 1), values)
        middle = range(1, pairs)
        if middle:
            for pair, response in zip(middle, convolve(g_one, 0, middle)):
                after_one(pair, response)

    def outer(low, high):
        project((0, pairs + 1), (low, high), (has_low, has_high))
        for pair, response in zip((0, pairs), convolve(g_one, 0, (0, pairs))):
            after_one(pair, response)

    def layer_two(q, current):
        (response,) = convolve(g_two, 1, (q,))
        halves = []
        for i in range(2):
            lanes = pl.ds((2 * q + 1 + i) * W, W)
            carried = g_two[pl.ds(HID, HID), lanes].astype(jnp.float32)
            halves.append((carried + activated(response, 1, i)).astype(jnp.bfloat16))
        network = jnp.dot(
            out_w[...], jnp.concatenate(halves, axis=1), preferred_element_type=jnp.float32
        )
        drift[q, 0:C, :] = push * network
        change = keep * current + drift[q]
        drift[q] = change
        return current + change

    def write(pair, value):
        for i in range(2):
            result[pl.ds(2 * pair + i, C, stride=R), :] = value[0:C, i * W : (i + 1) * W]

    loads[4].wait()
    inner([scaled[q] for q in range(pairs)])
    loads[5].wait()
    loads[6].wait()
    pl.when(has_low)(lambda: up(scaled.at[pairs - 1], *first).wait_recv())
    pl.when(has_high)(lambda: down(scaled.at[0], *first).wait_recv())
    outer(halo_one[0], halo_one[1])
    pl.when(has_next)(lambda: pl.semaphore_wait(ready, 1))
    for q in range(pairs):
        total = layer_two(q, own(q))

        @pl.when(slot == 0)
        def _():
            send_one[q] = total.astype(jnp.bfloat16)
            pl.when(has_next)(lambda: onward(q, *chain_one).start())
            write(q, total)

    for q in range(pairs):

        @pl.when(slot > 0)
        def _():
            onward(q, *chain_one).wait_recv()
            if q == 0:
                pl.when(has_low)(lambda: down(recv_one.at[0], *second).start())
            if q == pairs - 1:
                pl.when(has_high)(lambda: up(recv_one.at[pairs - 1], *second).start())
            send_one[q] = (recv_one[q].astype(jnp.float32) + drift[q]).astype(jnp.bfloat16)
            pl.when(has_next)(lambda: onward(q, *chain_one).start())

    @pl.when(slot > 0)
    def _():
        def state(q):
            return recv_one[q].astype(jnp.float32)

        def rescaled(value):
            return (value.astype(jnp.float32) * inverse).astype(jnp.bfloat16)

        inner([rescaled(recv_one[q]) for q in range(pairs)])
        pl.when(has_high)(lambda: down(recv_one.at[0], *second).wait_recv())
        pl.when(has_low)(lambda: up(recv_one.at[pairs - 1], *second).wait_recv())
        outer(rescaled(halo_two[0]), rescaled(halo_two[1]))
        for q in range(pairs):
            total = layer_two(q, state(q))

            @pl.when(slot == 1)
            def _():
                send_two[q] = total.astype(jnp.bfloat16)
                pl.when(has_next)(lambda: onward(q, *chain_two).start())
                write(q, total)

        for q in range(pairs):

            @pl.when(slot > 1)
            def _():
                onward(q, *chain_two).wait_recv()
                total = recv_two[q].astype(jnp.float32) + drift[q]
                send_two[q] = total.astype(jnp.bfloat16)
                pl.when(has_next)(lambda: onward(q, *chain_two).start())
                write(q, total)

    pl.when(has_low)(lambda: down(scaled.at[0], *first).wait_send())
    pl.when(has_high)(lambda: up(scaled.at[pairs - 1], *first).wait_send())

    @pl.when(has_next)
    def _():
        for q in range(pairs):
            onward(q, *chain_one).wait_send()

    @pl.when(slot > 0)
    def _():
        pl.when(has_low)(lambda: down(recv_one.at[0], *second).wait_send())
        pl.when(has_high)(lambda: up(recv_one.at[pairs - 1], *second).wait_send())

        @pl.when(has_next)
        def _():
            for q in range(pairs):
                onward(q, *chain_two).wait_send()


def on_device(times, bands, trajectory, step_levels, in_weight, in_bias, conv_weight, cond_weight, out_weight):
    _, C, R, W = trajectory.shape
    HID = in_weight.shape[0]
    pairs = R // 2
    padded = -(-C // 16) * 16
    wide = -(-C // 128) * 128
    bf16, f32 = jnp.bfloat16, jnp.float32
    block = (pairs, padded, 2 * W)
    halo = (2, padded, 2 * W)
    anywhere = pl.BlockSpec(memory_space=pltpu.HBM)
    dma = pltpu.SemaphoreType.DMA
    result = pl.pallas_call(
        functools.partial(kernel, (times, bands, C, R, W, HID)),
        out_shape=jax.ShapeDtypeStruct((C * R, W), f32),
        in_specs=[anywhere] * 7,
        out_specs=pl.BlockSpec(memory_space=pltpu.VMEM),
        scratch_shapes=[
            pltpu.SMEM(step_levels.shape, jnp.int32),
            pltpu.VMEM((padded * R, W), f32),
            pltpu.VMEM((C, HID), bf16),
            pltpu.VMEM((wide, HID), f32),
            pltpu.VMEM((HID, wide), bf16),
            pltpu.VMEM((1, HID), f32),
            pltpu.VMEM(conv_weight.shape, bf16),
            pltpu.VMEM(cond_weight.shape, bf16),
            pltpu.VMEM(out_weight.shape, bf16),
            pltpu.VMEM((4 * HID, W), f32),
            pltpu.VMEM((HID, W), f32),
            pltpu.VMEM((3 * HID, (R + 4) * W), bf16),
            pltpu.VMEM((3 * HID, (R + 2) * W), bf16),
            pltpu.VMEM(block, f32),
            pltpu.VMEM(block, bf16),
            pltpu.VMEM(halo, bf16),
            pltpu.VMEM(block, bf16),
            pltpu.VMEM(block, bf16),
            pltpu.VMEM(halo, bf16),
            pltpu.VMEM(block, bf16),
            pltpu.VMEM(block, bf16),
            dma((8,)),
            dma((2,)),
            dma((2,)),
            dma((pairs,)),
            dma((pairs,)),
            dma((2,)),
            dma((2,)),
            dma((pairs,)),
            dma((pairs,)),
            pltpu.SemaphoreType.REGULAR,
        ],
        compiler_params=pltpu.CompilerParams(
            collective_id=0, has_side_effects=True, vmem_limit_bytes=32 * 1024 * 1024
        ),
    )(
        *(
            pltpu.with_memory_space_constraint(operand, pltpu.HBM)
            for operand in (
                step_levels,
                trajectory.reshape(C * R, W),
                in_weight.T,
                in_bias.reshape(1, HID),
                conv_weight,
                cond_weight,
                out_weight,
            )
        ),
    )
    return result.reshape(1, C, R, W)


def solution(mesh):
    in_specs = (P("tm", None, "lat", None), P(), P(), P(), P(), P(), P())
    out_specs = P("tm", None, "lat", None)
    return jax.shard_map(
        functools.partial(on_device, mesh.shape["tm"], mesh.shape["lat"]),
        mesh=mesh,
        in_specs=in_specs,
        out_specs=out_specs,
        check_vma=False,
    )
```

```python
import functools

import jax
import jax.numpy as jnp
from jax import lax
from jax.experimental import pallas as pl
from jax.experimental.pallas import tpu as pltpu
from jax.sharding import PartitionSpec as P

LEVELS = 64
MESH = pl.DeviceIdType.MESH

sigma_top = 1.0
sigma_low = 0.02
rho_power = 7.0


def level_sigma(level):
    top, low = sigma_top ** (1.0 / rho_power), sigma_low ** (1.0 / rho_power)
    root = top + level.astype(jnp.float32) / (LEVELS - 1) * (low - top)
    square = root * root
    return square * square * square * root


def kernel(
    sizes,
    levels_hbm,
    x_hbm,
    in_hbm,
    bias_hbm,
    conv_hbm,
    cond_hbm,
    out_hbm,
    result,
    levels,
    xs,
    in_t,
    in_pad,
    in_w,
    bias_row,
    conv_w,
    cond_w,
    out_w,
    cond,
    bias,
    g_one,
    g_two,
    drift,
    scaled,
    halo_one,
    recv_one,
    send_one,
    halo_two,
    recv_two,
    send_two,
    load_sem,
    halo_one_s,
    halo_one_r,
    chain_one_s,
    chain_one_r,
    halo_two_s,
    halo_two_r,
    chain_two_s,
    chain_two_r,
):
    times, bands, C, R, W, HID = sizes
    pairs = R // 2
    W2 = 2 * W
    padded = scaled.shape[1]
    slot = lax.axis_index("tm")
    band = lax.axis_index("lat")
    has_low, has_high = band > 0, band < bands - 1
    has_next = slot < times - 1

    barrier = pltpu.get_barrier_semaphore()

    def greet(axis, index):
        pl.semaphore_signal(barrier, inc=1, device_id={axis: index}, device_id_type=MESH)

    pl.when(has_low)(lambda: greet("lat", band - 1))
    pl.when(has_high)(lambda: greet("lat", band + 1))
    pl.when(slot > 0)(lambda: greet("tm", slot - 1))

    loads = [
        pltpu.make_async_copy(source, target, load_sem.at[i])
        for i, (source, target) in enumerate(
            [
                (x_hbm, xs.at[pl.ds(0, C * R)]),
                (in_hbm, in_t),
                (bias_hbm, bias_row),
                (cond_hbm, cond_w),
                (conv_hbm.at[0], conv_w.at[0]),
                (conv_hbm.at[1], conv_w.at[1]),
                (out_hbm, out_w),
                (levels_hbm, levels),
            ]
        )
    ]
    for load in loads[-1:] + loads[:-1]:
        load.start()

    if padded > C:
        xs[C * R :, :] = jnp.zeros((padded * R - C * R, W), jnp.float32)

    loads[7].wait()
    sigma = level_sigma(jnp.full((1, W2), levels[slot], jnp.int32))
    sigma_next = level_sigma(jnp.full((1, W2), levels[slot + 1], jnp.int32))
    variance = sigma * sigma + 0.25
    inverse = 1.0 / jnp.sqrt(variance)
    gain = (sigma_next - sigma) / sigma
    keep = gain * (sigma * sigma / variance)
    push = -0.5 * gain * sigma * inverse

    def own(q):
        return jnp.concatenate(
            [xs[pl.ds(2 * q + i, padded, stride=R), :] for i in range(2)], axis=1
        )

    loads[0].wait()
    for q in range(pairs):
        scaled[q] = (own(q) * inverse).astype(jnp.bfloat16)

    def remote(source, target, send, receive, axis, index):
        return pltpu.make_async_remote_copy(
            src_ref=source,
            dst_ref=target,
            send_sem=send,
            recv_sem=receive,
            device_id={axis: index},
            device_id_type=MESH,
        )

    def down(source, halo, send, receive):
        return remote(source, halo.at[1], send.at[1], receive.at[1], "lat", band - 1)

    def up(source, halo, send, receive):
        return remote(source, halo.at[0], send.at[0], receive.at[0], "lat", band + 1)

    def onward(q, source, target, send, receive):
        return remote(
            source.at[q], target.at[q], send.at[q], receive.at[q], "tm", slot + 1
        )

    first = (halo_one, halo_one_s, halo_one_r)
    second = (halo_two, halo_two_s, halo_two_r)
    chain_one = (send_one, recv_one, chain_one_s, chain_one_r)
    chain_two = (send_two, recv_two, chain_two_s, chain_two_r)

    pl.semaphore_wait(
        barrier,
        has_low.astype(jnp.int32) + has_high.astype(jnp.int32) + has_next.astype(jnp.int32),
    )
    pl.when(has_low)(lambda: down(scaled.at[0], *first).start())
    pl.when(has_high)(lambda: up(scaled.at[pairs - 1], *first).start())

    drift[...] = jnp.zeros_like(drift)
    in_pad[...] = jnp.zeros_like(in_pad)
    loads[1].wait()
    loads[2].wait()
    in_pad[0:C, :] = in_t[...].astype(jnp.float32)
    for j in range(HID // W):
        rows = pl.ds(j * W, W)
        in_w[rows, :] = in_pad[:, j * W : (j + 1) * W].T.astype(jnp.bfloat16)
        bias[rows, :] = jnp.broadcast_to(bias_row[:, j * W : (j + 1) * W], (W, W)).T

    half = cond_w.shape[0] // 2
    place = lax.broadcasted_iota(jnp.int32, (1, half), 1).astype(jnp.float32) / half
    frequency = jnp.exp(place * jnp.log(jnp.full((1, half), 100.0, jnp.float32)))
    phases = jnp.log(sigma[:, :1]) / 4.0 * frequency
    embedding = jnp.concatenate([jnp.cos(phases), jnp.sin(phases)], axis=1)
    embedding = jnp.broadcast_to(embedding, (W, 2 * half)).astype(jnp.bfloat16)
    loads[3].wait()
    conditions = jnp.dot(embedding, cond_w[...], preferred_element_type=jnp.float32)
    for j in range(4 * HID // W):
        block = conditions[:, j * W : (j + 1) * W].T
        is_scale = (j * W // HID) % 2 == 0
        cond[pl.ds(j * W, W), :] = block + 1.0 if is_scale else block

    def shifts(target, chunk, halves):
        for i, half in enumerate(halves):
            lanes = pl.ds((2 * chunk + i) * W, W)
            value = half.astype(jnp.bfloat16)
            target[pl.ds(0, HID), lanes] = pltpu.roll(value, 1, 1)
            target[pl.ds(HID, HID), lanes] = value
            target[pl.ds(2 * HID, HID), lanes] = pltpu.roll(value, W - 1, 1)

    def project(chunks, values, insides=None):
        hidden = jnp.dot(
            in_w[:, :padded],
            jnp.concatenate(values, axis=1),
            preferred_element_type=jnp.float32,
        )
        for j, chunk in enumerate(chunks):
            halves = []
            for i in range(2):
                part = hidden[:, (2 * j + i) * W : (2 * j + i + 1) * W] + bias[...]
                halves.append(part if insides is None else jnp.where(insides[j], part, 0.0))
            shifts(g_one, chunk, halves)

    def convolve(source, layer, firsts):
        rows = [
            jnp.concatenate(
                [source[:, (2 * pair + a) * W : (2 * pair + a + 2) * W] for pair in firsts], axis=1
            )
            for a in range(3)
        ]
        response = jnp.dot(
            conv_w[layer], jnp.concatenate(rows, axis=0), preferred_element_type=jnp.float32
        )
        return [response[:, j * W2 : (j + 1) * W2] for j in range(len(firsts))]

    def activated(response, layer, i):
        scale = cond[pl.ds(2 * layer * HID, HID), :]
        shift = cond[pl.ds((2 * layer + 1) * HID, HID), :]
        value = response[:, i * W : (i + 1) * W] * scale + shift
        part = 0.5 * value
        return part + part * jnp.tanh(part)

    def after_one(pair, response):
        halves = [activated(response, 0, i) for i in range(2)]
        if pair == 0:
            halves[0] = jnp.where(has_low, halves[0], 0.0)
        if pair == pairs:
            halves[1] = jnp.where(has_high, halves[1], 0.0)
        shifts(g_two, pair, halves)

    def inner(values):
        project(range(1, pairs + 1), values)
        middle = range(1, pairs)
        if middle:
            for pair, response in zip(middle, convolve(g_one, 0, middle)):
                after_one(pair, response)

    def outer(low, high):
        project((0, pairs + 1), (low, high), (has_low, has_high))
        for pair, response in zip((0, pairs), convolve(g_one, 0, (0, pairs))):
            after_one(pair, response)

    def changes(current):
        halves = []
        for q, response in enumerate(convolve(g_two, 1, range(pairs))):
            for i in range(2):
                lanes = pl.ds((2 * q + 1 + i) * W, W)
                carried = g_two[pl.ds(HID, HID), lanes].astype(jnp.float32)
                halves.append((carried + activated(response, 1, i)).astype(jnp.bfloat16))
        network = jnp.dot(
            out_w[...], jnp.concatenate(halves, axis=1), preferred_element_type=jnp.float32
        )
        for q in range(pairs):
            drift[q, 0:C, :] = push * network[:, q * W2 : (q + 1) * W2]
        for q in range(pairs):
            yield q, keep * current(q) + drift[q]

    def write(pair, value):
        for i in range(2):
            result[pl.ds(2 * pair + i, C, stride=R), :] = value[0:C, i * W : (i + 1) * W]

    loads[4].wait()
    inner([scaled[q] for q in range(pairs)])
    loads[5].wait()
    loads[6].wait()
    pl.when(has_low)(lambda: up(scaled.at[pairs - 1], *first).wait_recv())
    pl.when(has_high)(lambda: down(scaled.at[0], *first).wait_recv())
    outer(halo_one[0], halo_one[1])
    for q, change in changes(own):

        @pl.when(slot == 0)
        def _():
            total = own(q) + change
            write(q, total)
            send_one[q] = total.astype(jnp.bfloat16)

        @pl.when(slot > 0)
        def _():
            onward(q, *chain_one).wait_recv()
            if q == 0:
                pl.when(has_low)(lambda: down(recv_one.at[0], *second).start())
            if q == pairs - 1:
                pl.when(has_high)(lambda: up(recv_one.at[pairs - 1], *second).start())
            send_one[q] = (recv_one[q].astype(jnp.float32) + change).astype(jnp.bfloat16)

        pl.when(has_next)(lambda: onward(q, *chain_one).start())

    @pl.when(slot > 0)
    def _():
        def state(q):
            return recv_one[q].astype(jnp.float32)

        def rescaled(value):
            return (value.astype(jnp.float32) * inverse).astype(jnp.bfloat16)

        inner([rescaled(recv_one[q]) for q in range(pairs)])
        pl.when(has_high)(lambda: down(recv_one.at[0], *second).wait_recv())
        pl.when(has_low)(lambda: up(recv_one.at[pairs - 1], *second).wait_recv())
        outer(rescaled(halo_two[0]), rescaled(halo_two[1]))
        for q, change in changes(state):

            @pl.when(slot == 1)
            def _():
                total = state(q) + change
                write(q, total)
                send_two[q] = total.astype(jnp.bfloat16)

            @pl.when(slot > 1)
            def _():
                onward(q, *chain_two).wait_recv()
                total = recv_two[q].astype(jnp.float32) + change
                write(q, total)
                send_two[q] = total.astype(jnp.bfloat16)

            pl.when(has_next)(lambda: onward(q, *chain_two).start())

    pl.when(has_low)(lambda: down(scaled.at[0], *first).wait_send())
    pl.when(has_high)(lambda: up(scaled.at[pairs - 1], *first).wait_send())

    @pl.when(has_next)
    def _():
        for q in range(pairs):
            onward(q, *chain_one).wait_send()

    @pl.when(slot > 0)
    def _():
        pl.when(has_low)(lambda: down(recv_one.at[0], *second).wait_send())
        pl.when(has_high)(lambda: up(recv_one.at[pairs - 1], *second).wait_send())

        @pl.when(has_next)
        def _():
            for q in range(pairs):
                onward(q, *chain_two).wait_send()


def on_device(times, bands, trajectory, step_levels, in_weight, in_bias, conv_weight, cond_weight, out_weight):
    _, C, R, W = trajectory.shape
    HID = in_weight.shape[0]
    pairs = R // 2
    padded = -(-C // 16) * 16
    wide = -(-C // 128) * 128
    bf16, f32 = jnp.bfloat16, jnp.float32
    block = (pairs, padded, 2 * W)
    halo = (2, padded, 2 * W)
    anywhere = pl.BlockSpec(memory_space=pltpu.HBM)
    dma = pltpu.SemaphoreType.DMA
    result = pl.pallas_call(
        functools.partial(kernel, (times, bands, C, R, W, HID)),
        out_shape=jax.ShapeDtypeStruct((C * R, W), f32),
        in_specs=[anywhere] * 7,
        out_specs=pl.BlockSpec(memory_space=pltpu.VMEM),
        scratch_shapes=[
            pltpu.SMEM(step_levels.shape, jnp.int32),
            pltpu.VMEM((padded * R, W), f32),
            pltpu.VMEM((C, HID), bf16),
            pltpu.VMEM((wide, HID), f32),
            pltpu.VMEM((HID, wide), bf16),
            pltpu.VMEM((1, HID), f32),
            pltpu.VMEM(conv_weight.shape, bf16),
            pltpu.VMEM(cond_weight.shape, bf16),
            pltpu.VMEM(out_weight.shape, bf16),
            pltpu.VMEM((4 * HID, W), f32),
            pltpu.VMEM((HID, W), f32),
            pltpu.VMEM((3 * HID, (R + 4) * W), bf16),
            pltpu.VMEM((3 * HID, (R + 2) * W), bf16),
            pltpu.VMEM(block, f32),
            pltpu.VMEM(block, bf16),
            pltpu.VMEM(halo, bf16),
            pltpu.VMEM(block, bf16),
            pltpu.VMEM(block, bf16),
            pltpu.VMEM(halo, bf16),
            pltpu.VMEM(block, bf16),
            pltpu.VMEM(block, bf16),
            dma((8,)),
            dma((2,)),
            dma((2,)),
            dma((pairs,)),
            dma((pairs,)),
            dma((2,)),
            dma((2,)),
            dma((pairs,)),
            dma((pairs,)),
        ],
        compiler_params=pltpu.CompilerParams(
            collective_id=0, has_side_effects=True, vmem_limit_bytes=32 * 1024 * 1024
        ),
    )(
        *(
            pltpu.with_memory_space_constraint(operand, pltpu.HBM)
            for operand in (
                step_levels,
                trajectory.reshape(C * R, W),
                in_weight.T,
                in_bias.reshape(1, HID),
                conv_weight,
                cond_weight,
                out_weight,
            )
        ),
    )
    return result.reshape(1, C, R, W)


def solution(mesh):
    in_specs = (P("tm", None, "lat", None), P(), P(), P(), P(), P(), P())
    out_specs = P("tm", None, "lat", None)
    return jax.shard_map(
        functools.partial(on_device, mesh.shape["tm"], mesh.shape["lat"]),
        mesh=mesh,
        in_specs=in_specs,
        out_specs=out_specs,
        check_vma=False,
    )
```
